256 devices in a mesh: region: 2 (over core), column: 4 (over x), layer: 32 (over z, y).
Axes of the slice: x: 4, y: 4, z: 8, core: 2. Of those that a mesh axis runs over, the one named last changes fastest.
Arguments:
- rhs: float32 [3, 256, 32, 512], P(None, 'layer', 'region', 'column'), may hold values from -0.8 to 0.8
- guess: float32 [3, 256, 32, 512], P(None, 'layer', 'region', 'column'), may hold values from -0.8 to 0.8
- diag_block: float32 [9, 256, 32, 512], P(None, 'layer', 'region', 'column'), may hold values from -4 to 4
- couple: float32 [3, 256, 32, 512], P(None, 'layer', 'region', 'column'), may hold values from 0.05 to 0.2
- pivot_inv: float32 [9, 256, 32, 512], P(None, 'layer', 'region', 'column')
- lower: float32 [9, 256, 32, 512], P(None, 'layer', 'region', 'column')
- upper: float32 [9, 256, 32, 512], P(None, 'layer', 'region', 'column')
- well_couple: float32 [9, 256, 32, 512], P(None, 'layer', 'region', 'column'), may hold values from -2 to 2
- well_inv: float32 [9, 16], replicated, may hold values from -0.0234375 to 0.0234375
- comp_tiles: int32 [32], replicated, may hold values from 0 to 127, as said below
- counts: int32 [16], replicated, may hold values from 0 to 16, as said below
Outputs:
- preconditioned: float32 [3, 256, 32, 512], P(None, 'layer', 'region', 'column')
The draws below stay inside these ranges and needn't reach their ends.
Inputs may be any that keep to these rules, and one draw needn't show every extreme that they name: `comp_tiles`: well w is owned by the device with index w % 8 over region and column. Each device over region and column has exactly 4 perforated tiles, on distinct rows; they go in groups of exactly 2 to 2 distinct owners; no tile is listed twice; lists are sorted by well and within a well by tile id. The counts sum to 32; a well has at most 2 tiles of any one device.
All inputs are finite; a program needn't handle non-finite values.
Results may differ from the reference program's by a relative error of at most 0.00016.
Values sent between devices are 32-bit elements; how exact they have to be, the bound alone decides.
No kernel may reach another device: no remote copies, remote signals or barrier semaphores. Data moves between devices by JAX's collectives and lax.ppermute only.
A program may use at most 64 MiB of HBM per device.

```python
import jax
import jax.numpy as jnp
from jax import lax

CX = 16
CY = 128
CZ = 8
CAP = 2
PERF_DEV = 4
WELLS_DEV = 2
AREAS = 8
NW = 16
NPERF = 32
NX = 32
NY = 512
LAYER_COUNT = 256
N_COLUMN = 4
N_LAYER = 32


def build_system(diag, offset_index):
    return jnp.stack([diag[0], offset_index[0], offset_index[1], offset_index[2], diag[1], offset_index[3], offset_index[4], offset_index[5], diag[2]])


def coupling(key, fast_share, spread):
    sort_keys = jax.random.split(key, 7)
    cell_shape = (3, 1, NX, NY)
    slow = jax.random.uniform(sort_keys[0], cell_shape, jnp.float32, 0.985, 1.0)
    fast = jax.random.uniform(sort_keys[1], cell_shape, jnp.float32, 0.5, 0.9)
    flow_rate = jnp.where(jax.random.uniform(sort_keys[2], cell_shape) < fast_share, fast, slow)
    perforation_group = jnp.where(jax.random.uniform(sort_keys[3], (1, LAYER_COUNT, 1, 1)) < 0.05, jax.random.uniform(sort_keys[4], (1, LAYER_COUNT, 1, 1), jnp.float32, 0.5, 0.8), 1.0)
    coarse_estimate = jax.random.uniform(sort_keys[5], (3, LAYER_COUNT, NX, NY), jnp.float32, 0.97, 1.0)
    offset_index = spread * jax.random.normal(sort_keys[6], (6, LAYER_COUNT, NX, NY), jnp.float32)
    return -build_system(flow_rate * perforation_group * coarse_estimate, offset_index)


def draw_lower(key, part):
    key = jax.random.fold_in(key, 11)
    return coupling(key, 0.5, 0.04)


def draw_upper(key, part):
    key = jax.random.fold_in(key, 12)
    return coupling(key, 0.5, 0.04)


def draw_pivot_inv(key, part):
    key = jax.random.fold_in(key, 13)
    first, second = jax.random.split(key)
    diag = jax.random.uniform(first, (3, LAYER_COUNT, NX, NY), jnp.float32, 0.97, 1.0)
    offset_index = 0.03 * jax.random.normal(second, (6, LAYER_COUNT, NX, NY), jnp.float32)
    return build_system(diag, offset_index)


def partial_rows(key):
    return jax.random.permutation(key, CX)


def well_layout(key):
    k_pick, k_rows, k_well = jax.random.split(key, 3)
    groups = PERF_DEV // CAP
    favour = (AREAS - jnp.arange(AREAS, dtype=jnp.int32)) * 4096
    first_owner = jnp.where(jnp.arange(AREAS, dtype=jnp.int32) == 0, 8192 * AREAS, 0).astype(jnp.int32)
    scores = jax.random.randint(k_pick, (AREAS, AREAS), 0, 4096 * AREAS) + favour[None, :] + first_owner[None, :]
    scores = scores * AREAS + jnp.arange(AREAS, dtype=jnp.int32)[None, :]
    chosen = lax.top_k(scores, groups)[1].astype(jnp.int32)
    row_keys = jax.random.split(k_rows, AREAS)
    rows = jax.vmap(partial_rows)(row_keys)[:, :PERF_DEV].astype(jnp.int32)
    owner_of = jnp.repeat(chosen, CAP, axis=1)
    later = (jnp.arange(PERF_DEV, dtype=jnp.int32) >= CAP).astype(jnp.int32)
    choose = jax.random.randint(k_well, (AREAS, PERF_DEV), 0, WELLS_DEV) * later[None, :]
    well_of = (owner_of + AREAS * choose).astype(jnp.int32)
    tile = jnp.arange(AREAS, dtype=jnp.int32)[:, None] * CX + rows
    order = jnp.argsort((well_of * (AREAS * CX) + tile).reshape(-1))
    comp = tile.reshape(-1)[order].astype(jnp.int32)
    counts = jnp.sum((well_of.reshape(-1)[:, None] == jnp.arange(NW, dtype=jnp.int32)[None, :]).astype(jnp.int32), axis=0)
    return (comp, counts)


def draw_comp_tiles(key, part):
    return well_layout(key)[0]


def draw_counts(key, part):
    return well_layout(key)[1]


def block_scale(stream_key, extent, shards, low, largest):
    def one(position, blocks):
        heights = jax.random.uniform(jax.random.fold_in(jax.random.fold_in(stream_key, 6), position), (blocks,), jnp.float32, low / len(shards), largest / len(shards))
        return jnp.repeat(jnp.exp(heights), extent[position] // blocks).reshape((-1,) + (1,) * (len(extent) - position - 1))

    factor_of = one(*shards[0])
    for cut in shards[1:]:
        factor_of = factor_of * one(*cut)
    return factor_of


def noise(key, shape, width, bound, cuts=(), kind=jnp.bfloat16):
    entries = jax.random.normal(key, shape, jnp.float32) * width
    if len(cuts) > 0:
        entries = block_scale(key, shape, cuts, -0.22, 0.18) * entries
    return jnp.clip(entries, min=-bound, max=bound).astype(kind)


def setup_inputs(seed: int = 0) -> dict:
    keys = jax.random.split(jax.random.key(seed), 12)
    return {
        "rhs": noise(keys[0], (3, LAYER_COUNT, NX, NY), 0.1, 0.8, ((1, 32), (2, 2), (3, 4)), jnp.float32),
        "guess": noise(keys[1], (3, LAYER_COUNT, NX, NY), 0.1, 0.8, ((1, 32), (2, 2), (3, 4)), jnp.float32),
        "diag_block": noise(keys[2], (9, LAYER_COUNT, NX, NY), 0.6, 4.0, ((1, 32), (2, 2), (3, 4)), jnp.float32),
        "couple": jnp.clip(0.05 + 0.15 * jax.random.uniform(keys[3], (3, LAYER_COUNT, NX, NY), jnp.float32) ** block_scale(keys[3], (3, LAYER_COUNT, NX, NY), ((1, 32), (2, 2), (3, 4)), -0.2, 0.2), 0.05, 0.2),
        "pivot_inv": draw_pivot_inv(jax.random.fold_in(keys[11], 71), 0),
        "lower": draw_lower(jax.random.fold_in(keys[11], 71), 0),
        "upper": draw_upper(jax.random.fold_in(keys[11], 71), 0),
        "well_couple": noise(keys[7], (9, LAYER_COUNT, NX, NY), 0.3, 2.0, ((1, 32), (2, 2), (3, 4)), jnp.float32),
        "well_inv": noise(keys[8], (9, NW), (CZ * CY * N_LAYER * NPERF // NW) ** -0.5, 0.0234375, (), jnp.float32),
        "comp_tiles": draw_comp_tiles(jax.random.fold_in(keys[11], 71), 0),
        "counts": draw_counts(jax.random.fold_in(keys[11], 71), 0),
    }


def block_mix(blk, vec):
    return jnp.stack([blk[3 * i] * vec[0] + blk[3 * i + 1] * vec[1] + blk[3 * i + 2] * vec[2] for i in range(3)])


def block_mix_t(blk, vec):
    return jnp.stack([blk[j] * vec[0] + blk[3 + j] * vec[1] + blk[6 + j] * vec[2] for j in range(3)])


def layers_first(array):
    return jnp.moveaxis(array, 1, 0)


def reference(rhs, guess, diag_block, couple, pivot_inv, lower, upper, well_couple, well_inv, comp_tiles, counts):
    padded = jnp.pad(guess, ((0, 0), (1, 1), (1, 1), (1, 1)))
    beside = padded[:, 2:, 1:-1, 1:-1] + padded[:, :-2, 1:-1, 1:-1]
    beside = beside + padded[:, 1:-1, 2:, 1:-1] + padded[:, 1:-1, :-2, 1:-1]
    beside = beside + padded[:, 1:-1, 1:-1, 2:] + padded[:, 1:-1, 1:-1, :-2]
    resid = rhs - (block_mix(diag_block, guess) - couple * beside)

    def going_down(prev, layer):
        pinv, low, res = layer
        now = block_mix(pinv, res - block_mix(low, prev))
        return now, now

    def going_up(prev, layer):
        pinv, upp, value = layer
        now = value - block_mix(pinv, block_mix(upp, prev))
        return now, now

    start = jnp.zeros((3, NX, NY), jnp.float32)
    unused, forward = lax.scan(going_down, start, (layers_first(pivot_inv), layers_first(lower), layers_first(resid)))
    unused, backward = lax.scan(going_up, start, (layers_first(pivot_inv), layers_first(upper), forward), reverse=True)
    solved = jnp.moveaxis(backward, 0, 1)

    products = block_mix(well_couple, solved)
    tile_sums = jnp.sum(products.reshape(3, LAYER_COUNT, NX, N_COLUMN, CY), axis=(1, 4))
    ends = jnp.cumsum(counts).astype(jnp.int32)
    place = jnp.arange(NPERF, dtype=jnp.int32)
    well_of = jnp.sum((place[:, None] >= ends[None, :]).astype(jnp.int32), axis=1)
    area = comp_tiles // CX
    row_x = (area // N_COLUMN) * CX + comp_tiles % CX
    block_y = area % N_COLUMN
    values = tile_sums[:, row_x, block_y]
    totals = jax.ops.segment_sum(values.T, well_of, num_segments=NW)
    rates = jnp.stack([well_inv[3 * i] * totals[:, 0] + well_inv[3 * i + 1] * totals[:, 1] + well_inv[3 * i + 2] * totals[:, 2] for i in range(3)])
    tile_rate = jnp.zeros((3, NX, N_COLUMN), jnp.float32).at[:, row_x, block_y].add(rates[:, well_of])
    cell_rate = jnp.broadcast_to(tile_rate[:, None, :, :, None], (3, LAYER_COUNT, NX, N_COLUMN, CY)).reshape(3, LAYER_COUNT, NX, NY)
    return solved - block_mix_t(well_couple, cell_rate)
```

```python
import jax
import jax.numpy as jnp
from jax import lax
from jax.experimental import pallas as pl
from jax.experimental.pallas import tpu as pltpu
from jax.sharding import PartitionSpec as P

AREA = ("region", "column")
DEPTH, ROWS, LANES = 8, 16, 128
HALF = LANES // 2
PACK = 48
BACK = 8

LEFT = {"lower": 0, "state": 9, "pivot": 18, "well": 27, "source": 36, "couple": 39, "guess": 42}
RIGHT = {"upper": 0, "cross": 9, "state": 18, "well": 27, "source": 36, "couple": 39, "guess": 42}


def mat(a, b):
    return [
        a[3 * i] * b[m] + a[3 * i + 1] * b[3 + m] + a[3 * i + 2] * b[6 + m]
        for i in range(3)
        for m in range(3)
    ]


def vec(a, x):
    return [a[3 * i] * x[0] + a[3 * i + 1] * x[1] + a[3 * i + 2] * x[2] for i in range(3)]


def neg(a):
    return [-entry for entry in a]


def add(a, b):
    return [x + y for x, y in zip(a, b)]


def sub(a, b):
    return [x - y for x, y in zip(a, b)]


def iota(shape, axis):
    return lax.broadcasted_iota(jnp.int32, shape, axis)


def edges_kernel(guess, x_out, right_out, left_out):
    region = lax.axis_index("region")
    lane = iota((ROWS, LANES), 1)
    right = jnp.zeros((ROWS, LANES), jnp.float32)
    left = jnp.zeros((ROWS, LANES), jnp.float32)
    for c in range(3):
        for k in range(DEPTH):
            place = c * DEPTH + k
            block = guess[c, k]
            right = jnp.where(lane == place, pltpu.roll(block, (place + 1) % LANES, 1), right)
            left = jnp.where(lane == place, pltpu.roll(block, place, 1) if place else block, left)
            x_out[place : place + 1, :] = jnp.where(
                region == 0, guess[c, k, ROWS - 1 :, :], guess[c, k, :1, :]
            )
    right_out[...] = right
    left_out[...] = left


def maps_kernel(
    x_in, right_in, left_in, rhs, guess, diag, couple, pivot, lower, upper, well,
    send, cross_out, state_out, trial_out, well_out, forward, states,
):
    region = lax.axis_index("region")
    column = lax.axis_index("column")
    n_column = lax.axis_size("column")
    lane = iota((8, LANES), 1)
    row = iota((8, LANES), 0)
    is_left = lane < HALF
    well_sums = jnp.zeros((8, LANES), jnp.float32)
    for h in range(2):
        at = slice(8 * h, 8 * h + 8)

        def load(ref, k, count):
            return [ref[c, k, at, :] for c in range(count)]

        edge_right = jnp.where(column > 0, right_in[at, :], 0.0)
        edge_left = jnp.where(column < n_column - 1, left_in[at, :], 0.0)

        def residual(k):
            mid = load(guess, k, 3)
            out = vec(load(diag, k, 9), mid)
            for c in range(3):
                g = mid[c]
                place = c * DEPTH + k
                x_row = x_in[place : place + 1, :]
                if h == 0:
                    outer = jnp.where(region > 0, x_row, 0.0)
                    below = jnp.where(row == 0, outer, pltpu.roll(g, 1, 0))
                    above = guess[c, k, 1:9, :]
                else:
                    outer = jnp.where(region == 0, x_row, 0.0)
                    below = guess[c, k, 7:15, :]
                    above = jnp.where(row == 7, outer, pltpu.roll(g, 7, 0))
                first = pltpu.roll(edge_right, LANES - place, 1) if place else edge_right
                before = jnp.where(lane == 0, first, pltpu.roll(g, 1, 1))
                last = pltpu.roll(edge_left, LANES - 1 - place, 1)
                after = jnp.where(lane == LANES - 1, last, pltpu.roll(g, LANES - 1, 1))
                beside = below + above + before + after
                if k > 0:
                    beside = beside + guess[c, k - 1, at, :]
                if k < DEPTH - 1:
                    beside = beside + guess[c, k + 1, at, :]
                out[c] = rhs[c, k, at, :] - (out[c] - couple[c, k, at, :] * beside)
            return out

        f = None
        big_f = None
        for k in range(DEPTH):
            res = residual(k)
            pinv = load(pivot, k, 9)
            if k == 0:
                f = vec(pinv, res)
                big_f = pinv
            else:
                low = load(lower, k, 9)
                f = vec(pinv, sub(res, vec(low, f)))
                big_f = neg(mat(pinv, mat(low, big_f)))
            for c in range(3):
                forward[c, k] = f[c]
            for c in range(9):
                states[c, k] = big_f[c]

        def put(place, left, right):
            low_cols = jnp.where(is_left, left, pltpu.roll(right, HALF, 1))
            high_cols = jnp.where(is_left, pltpu.roll(left, HALF, 1), right)
            send[pl.ds(16 * h * PACK + place, 8, 2 * PACK), :] = low_cols
            send[pl.ds((16 * h + 1) * PACK + place, 8, 2 * PACK), :] = high_cols

        top = DEPTH - 1
        s, cross, state = f, big_f, load(pivot, top, 9)
        coef = load(well, top, 9)
        well_state, well_cross, well_const = mat(coef, state), mat(coef, cross), vec(coef, s)
        for k in reversed(range(DEPTH)):
            if k < top:
                both = mat(load(pivot, k, 9), load(upper, k, 9))
                s = sub([forward[c, k] for c in range(3)], vec(both, s))
                cross = sub([states[c, k] for c in range(9)], mat(both, cross))
                state = neg(mat(both, state))
                coef = load(well, k, 9)
                well_state = add(well_state, mat(coef, state))
                well_cross = add(well_cross, mat(coef, cross))
                well_const = add(well_const, vec(coef, s))
            for c in range(3):
                trial_out[c, k, at, :] = s[c]
            for c in range(9):
                cross_out[c, k, at, :] = cross[c]
                state_out[c, k, at, :] = state[c]

        for e in range(9):
            put(e, lower[e, 0, at, :], upper[e, top, at, :])
            put(9 + e, states[e, top], cross[e])
            put(18 + e, pivot[e, top, at, :], state[e])
            put(27 + e, well_cross[e], well_state[e])
        for c in range(3):
            put(36 + c, forward[c, top], s[c])
            put(39 + c, couple[c, 0, at, :], couple[c, top, at, :])
            put(42 + c, guess[c, top, at, :], guess[c, 0, at, :])
            total = jnp.sum(well_const[c], axis=1, keepdims=True)
            well_sums = well_sums + jnp.where(lane == c * ROWS + 8 * h + row, total, 0.0)
        for place in range(45, PACK):
            put(place, jnp.zeros((8, LANES), jnp.float32), jnp.zeros((8, LANES), jnp.float32))
    well_out[...] = jnp.broadcast_to(jnp.sum(well_sums, axis=0, keepdims=True), (8, LANES))


def chain_kernel(peers, got, well_sums, send, step_ref, base_ref, inflow_ref):
    layer = lax.axis_index("layer")
    lane = iota((peers, LANES), 1)
    row = iota((peers, LANES), 0)
    is_left = lane < HALF

    def take(place, count):
        return [got[pl.ds(place + e, peers, PACK), :] for e in range(count)]

    def swap(a):
        return [pltpu.roll(entry, HALF, 1) for entry in a]

    def chain(step, base, order):
        for e in range(9):
            step_ref[e] = step[e]
        for c in range(3):
            base_ref[c] = base[c]
        x = [jnp.zeros((1, LANES), jnp.float32)] * 3
        for d in order:
            at = slice(d, d + 1)
            for c in range(3):
                inflow_ref[c, at, :] = x[c]
            x = sub([base_ref[c, at, :] for c in range(3)], vec([step_ref[e, at, :] for e in range(9)], x))
        return [inflow_ref[c] for c in range(3)]

    edge = take(0, 9)
    states = take(9, 9)
    pivots = take(18, 9)
    source = take(36, 3)
    couple = take(39, 3)
    guess = take(42, 3)
    from_below = [jnp.where(row == 0, 0.0, pltpu.roll(g, 1, 0)) for g in guess]
    from_above = [jnp.where(row == peers - 1, 0.0, pltpu.roll(g, peers - 1, 0)) for g in guess]
    near = [c * jnp.where(is_left, b, a) for c, b, a in zip(couple, from_below, from_above)]
    above = swap(near)
    base = add(add(source, vec(pivots, above)), vec(states, near))
    step = mat(states, edge)
    f_in = chain(step, base, range(peers))
    u = sub(near, vec(edge, f_in))
    up_base = add(add(source, vec(states, swap(u))), vec(pivots, near))
    s_in = chain(mat(pivots, edge), up_base, reversed(range(peers)))
    w = sub(near, vec(edge, s_in))
    both = [jnp.where(is_left, a, b) for a, b in zip(u, w)]
    parts = vec(take(27, 9), both)
    mine = well_sums[0:1, :]
    one = iota((1, LANES), 1)
    for c in range(3):
        total = jnp.sum(jnp.sum(parts[c], axis=0, keepdims=True), axis=1, keepdims=True)
        mine = mine + jnp.where(one == c * ROWS + layer // 2, total, 0.0)
        send[pl.ds(c, peers, BACK), :] = both[c]
    send[pl.ds(3, peers, BACK), :] = jnp.broadcast_to(mine, (peers, LANES))
    for place in range(4, BACK):
        send[pl.ds(place, peers, BACK), :] = jnp.zeros((peers, LANES), jnp.float32)


def solved_kernel(areas, peers, got, cross, state, trial, solved, sums):
    is_left = iota((ROWS, LANES), 1) < HALF
    u, w = [], []
    for c in range(3):
        low_cols = got[pl.ds(c, ROWS, 2 * BACK), :]
        high_cols = got[pl.ds(BACK + c, ROWS, 2 * BACK), :]
        u.append(jnp.where(is_left, low_cols, pltpu.roll(high_cols, HALF, 1)))
        w.append(jnp.where(is_left, pltpu.roll(low_cols, HALF, 1), high_cols))
    total = jnp.sum(got[pl.ds(3, peers, BACK), :], axis=0, keepdims=True)
    sums[...] = jnp.broadcast_to(total, (8 * areas, LANES))
    for k in range(DEPTH):
        part = add(vec([cross[e, k] for e in range(9)], u), vec([state[e, k] for e in range(9)], w))
        for c in range(3):
            solved[c, k] = trial[c, k] + part[c]


def wells_kernel(areas, nperf, nwell, tiles, counts, inverse, sums, solved, well, out):
    me = lax.axis_index("region") * lax.axis_size("column") + lax.axis_index("column")
    lane = iota((areas, LANES), 1)
    tile_all = iota((areas, LANES), 0) * ROWS + lane % ROWS
    tile_own = me * ROWS + iota((ROWS, LANES), 0)
    place_all = jnp.full((areas, LANES), -1, jnp.int32)
    place_own = jnp.full((ROWS, LANES), -1, jnp.int32)
    for p in range(nperf):
        place_all = jnp.where(tile_all == tiles[p], p, place_all)
        place_own = jnp.where(tile_own == tiles[p], p, place_own)
    well_all = jnp.where(place_all < 0, -1, 0)
    well_own = jnp.where(place_own < 0, -2, 0)
    end = 0
    for w in range(nwell):
        end = end + counts[w]
        well_all = well_all + (place_all >= end).astype(jnp.int32)
        well_own = well_own + (place_own >= end).astype(jnp.int32)
    gathered = jnp.zeros((ROWS, LANES), jnp.float32)
    for a in range(areas):
        same = well_own == well_all[a : a + 1, :]
        gathered = gathered + jnp.where(same, sums[8 * a : 8 * a + 1, :], 0.0)
    wide = iota((ROWS, LANES), 1)
    totals = [
        jnp.sum(
            jnp.where((wide >= c * ROWS) & (wide < (c + 1) * ROWS), gathered, 0.0),
            axis=1,
            keepdims=True,
        )
        for c in range(3)
    ]
    block = []
    for e in range(9):
        entry = jnp.zeros((ROWS, LANES), jnp.float32)
        for w in range(nwell):
            entry = jnp.where(well_own == w, inverse[e, w], entry)
        block.append(entry)
    rate = vec(block, totals)
    for k in range(DEPTH):
        for c in range(3):
            out[c, k] = solved[c, k] - (
                well[c, k] * rate[0] + well[3 + c, k] * rate[1] + well[6 + c, k] * rate[2]
            )


def f32(*shape):
    return jax.ShapeDtypeStruct(shape, jnp.float32)


def call(kernel, out_shape, scratch=(), in_specs=None):
    extra = {} if in_specs is None else {"in_specs": in_specs}
    return pl.pallas_call(
        kernel,
        out_shape=out_shape,
        scratch_shapes=scratch,
        compiler_params=pltpu.CompilerParams(vmem_limit_bytes=40 * 1024 * 1024),
        **extra,
    )


def moved(value, axis, by):
    count = lax.axis_size(axis)
    return lax.ppermute(value, axis, [(i, (i + by) % count) for i in range(count)])


def exchanged(value, axes):
    return lax.all_to_all(value, axes, split_axis=0, concat_axis=0, tiled=True)


def local(rhs, guess, diag, couple, pivot, lower, upper, well, inverse, tiles, counts):
    peers = lax.axis_size("layer")
    areas = lax.axis_size(AREA)
    cells = (DEPTH, ROWS, LANES)
    x_face, right_face, left_face = call(
        edges_kernel, (f32(3 * DEPTH, LANES), f32(ROWS, LANES), f32(ROWS, LANES))
    )(guess)
    right_in = moved(right_face, "column", 1)
    left_in = moved(left_face, "column", -1)
    x_in = moved(x_face, "region", 1)
    send, cross, state, trial, well_sums = call(
        maps_kernel,
        (f32(peers * PACK, LANES), f32(9, *cells), f32(9, *cells), f32(3, *cells), f32(8, LANES)),
        [pltpu.VMEM((3, DEPTH, 8, LANES), jnp.float32), pltpu.VMEM((9, DEPTH, 8, LANES), jnp.float32)],
    )(x_in, right_in, left_in, rhs, guess, diag, couple, pivot, lower, upper, well)
    got = exchanged(send.reshape(peers, PACK, LANES), "layer").reshape(peers * PACK, LANES)
    back = call(
        lambda *refs: chain_kernel(peers, *refs),
        f32(peers * BACK, LANES),
        [
            pltpu.VMEM((9, peers, LANES), jnp.float32),
            pltpu.VMEM((3, peers, LANES), jnp.float32),
            pltpu.VMEM((3, peers, LANES), jnp.float32),
        ],
    )(got, well_sums)
    got = exchanged(back.reshape(peers, BACK, LANES), "layer").reshape(peers * BACK, LANES)
    solved, sums = call(
        lambda *refs: solved_kernel(areas, peers, *refs), (f32(3, *cells), f32(8 * areas, LANES))
    )(got, cross, state, trial)
    sums = exchanged(sums.reshape(areas, 8, LANES), AREA).reshape(8 * areas, LANES)
    vmem = pl.BlockSpec(memory_space=pltpu.VMEM)
    smem = pl.BlockSpec(memory_space=pltpu.SMEM)
    return call(
        lambda *refs: wells_kernel(areas, tiles.shape[0], counts.shape[0], *refs),
        f32(3, *cells),
        in_specs=[smem, smem, smem, vmem, vmem, vmem],
    )(tiles, counts, inverse, sums, solved, well)


def solution(mesh):
    cells = P(None, "layer", "region", "column")
    return jax.shard_map(
        local,
        mesh=mesh,
        in_specs=(cells,) * 8 + (P(),) * 3,
        out_specs=cells,
        check_vma=False,
    )
```

```python
import jax
import jax.numpy as jnp
from jax import lax
from jax.experimental import pallas as pl
from jax.experimental.pallas import tpu as pltpu
from jax.sharding import PartitionSpec as P

AREA = ("region", "column")
DEPTH, ROWS, LANES = 8, 16, 128
HALF = LANES // 2
PACK = 32
BACK = 8

STEP, MIXED, WELL, SOURCE = 0, 9, 18, 27


def mat(a, b):
    return [
        a[3 * i] * b[m] + a[3 * i + 1] * b[3 + m] + a[3 * i + 2] * b[6 + m]
        for i in range(3)
        for m in range(3)
    ]


def vec(a, x):
    return [a[3 * i] * x[0] + a[3 * i + 1] * x[1] + a[3 * i + 2] * x[2] for i in range(3)]


def neg(a):
    return [-entry for entry in a]


def add(a, b):
    return [x + y for x, y in zip(a, b)]


def sub(a, b):
    return [x - y for x, y in zip(a, b)]


def iota(shape, axis):
    return lax.broadcasted_iota(jnp.int32, shape, axis)


def edges_kernel(guess, x_out, right_out, left_out, top_out, bottom_out):
    region = lax.axis_index("region")
    lane = iota((ROWS, LANES), 1)
    right = jnp.zeros((ROWS, LANES), jnp.float32)
    left = jnp.zeros((ROWS, LANES), jnp.float32)
    for c in range(3):
        for k in range(DEPTH):
            place = c * DEPTH + k
            block = guess[c, k]
            right = jnp.where(lane == place, pltpu.roll(block, (place + 1) % LANES, 1), right)
            left = jnp.where(lane == place, pltpu.roll(block, place, 1) if place else block, left)
            x_out[place : place + 1, :] = jnp.where(
                region == 0, guess[c, k, ROWS - 1 :, :], guess[c, k, :1, :]
            )
        top_out[c] = guess[c, DEPTH - 1]
        bottom_out[c] = guess[c, 0]
    right_out[...] = right
    left_out[...] = left


def put(send, h, place, left, right):
    is_left = iota((8, LANES), 1) < HALF
    low_cols = jnp.where(is_left, left, pltpu.roll(right, HALF, 1))
    high_cols = jnp.where(is_left, pltpu.roll(left, HALF, 1), right)
    send[pl.ds(16 * h * PACK + place, 8, 2 * PACK), :] = low_cols
    send[pl.ds((16 * h + 1) * PACK + place, 8, 2 * PACK), :] = high_cols


def well_masks(areas, nperf, nwell, tiles, counts, inverse, same_out, block_out):
    me = lax.axis_index("region") * lax.axis_size("column") + lax.axis_index("column")
    tile_all = iota((areas, LANES), 0) * ROWS + iota((areas, LANES), 1) % ROWS
    tile_own = me * ROWS + iota((ROWS, LANES), 0)
    place_all = jnp.full((areas, LANES), -1, jnp.int32)
    place_own = jnp.full((ROWS, LANES), -1, jnp.int32)
    for p in range(nperf):
        place_all = jnp.where(tile_all == tiles[p], p, place_all)
        place_own = jnp.where(tile_own == tiles[p], p, place_own)
    well_all = jnp.where(place_all < 0, -1, 0)
    well_own = jnp.where(place_own < 0, -2, 0)
    end = 0
    for w in range(nwell):
        end = end + counts[w]
        well_all = well_all + (place_all >= end).astype(jnp.int32)
        well_own = well_own + (place_own >= end).astype(jnp.int32)
    for a in range(areas):
        same_out[a] = (well_own == well_all[a : a + 1, :]).astype(jnp.float32)
    for e in range(9):
        entry = jnp.zeros((ROWS, LANES), jnp.float32)
        for w in range(nwell):
            entry = jnp.where(well_own == w, inverse[e, w], entry)
        block_out[e] = entry


def maps_kernel(
    areas, nperf, nwell,
    tiles, counts, inverse, pivot, lower, upper, well,
    send, cross_out, state_out, same_out, block_out, states,
):
    well_masks(areas, nperf, nwell, tiles, counts, inverse, same_out, block_out)
    top = DEPTH - 1
    for h in range(2):
        at = slice(8 * h, 8 * h + 8)

        def load(ref, k):
            return [ref[c, k, at, :] for c in range(9)]

        state = None
        for k in range(DEPTH):
            low = load(lower, k)
            state = neg(mat(load(pivot, k), low if k == 0 else mat(low, state)))
            for c in range(9):
                states[c, k] = state[c]
        down = state
        cross = state
        well_state, well_cross = None, None
        for k in reversed(range(DEPTH)):
            both = mat(load(pivot, k), load(upper, k))
            if k == top:
                state = neg(both)
            else:
                cross = sub([states[c, k] for c in range(9)], mat(both, cross))
                state = neg(mat(both, state))
            coef = load(well, k)
            more_state, more_cross = mat(coef, state), mat(coef, cross)
            well_state = more_state if k == top else add(well_state, more_state)
            well_cross = more_cross if k == top else add(well_cross, more_cross)
            for c in range(9):
                cross_out[c, k, at, :] = cross[c]
                state_out[c, k, at, :] = state[c]
        zero = jnp.zeros((8, LANES), jnp.float32)
        for e in range(9):
            put(send, h, STEP + e, down[e], state[e])
            put(send, h, MIXED + e, well_cross[e], cross[e])
            put(send, h, WELL + e, zero, well_state[e])
        for place in range(30, PACK):
            put(send, h, place, zero, zero)


def trial_kernel(
    x_in, right_in, left_in, below_in, above_in, rhs, guess, diag, couple, pivot, lower, upper, well, sent,
    send, trial_out, well_out, forward,
):
    region = lax.axis_index("region")
    column = lax.axis_index("column")
    layer = lax.axis_index("layer")
    n_column = lax.axis_size("column")
    n_layer = lax.axis_size("layer")
    lane = iota((8, LANES), 1)
    row = iota((8, LANES), 0)
    top = DEPTH - 1
    well_sums = jnp.zeros((8, LANES), jnp.float32)
    for h in range(2):
        at = slice(8 * h, 8 * h + 8)

        def load(ref, k, count=9):
            return [ref[c, k, at, :] for c in range(count)]

        edge_right = jnp.where(column > 0, right_in[at, :], 0.0)
        edge_left = jnp.where(column < n_column - 1, left_in[at, :], 0.0)

        def residual(k):
            mid = load(guess, k, 3)
            out = vec(load(diag, k), mid)
            for c in range(3):
                g = mid[c]
                place = c * DEPTH + k
                x_row = x_in[place : place + 1, :]
                if h == 0:
                    outer = jnp.where(region > 0, x_row, 0.0)
                    below = jnp.where(row == 0, outer, pltpu.roll(g, 1, 0))
                    above = guess[c, k, 1:9, :]
                else:
                    outer = jnp.where(region == 0, x_row, 0.0)
                    below = guess[c, k, 7:15, :]
                    above = jnp.where(row == 7, outer, pltpu.roll(g, 7, 0))
                first = pltpu.roll(edge_right, LANES - place, 1) if place else edge_right
                before = jnp.where(lane == 0, first, pltpu.roll(g, 1, 1))
                last = pltpu.roll(edge_left, LANES - 1 - place, 1)
                after = jnp.where(lane == LANES - 1, last, pltpu.roll(g, LANES - 1, 1))
                beside = below + above + before + after
                if k > 0:
                    beside = beside + guess[c, k - 1, at, :]
                else:
                    beside = beside + jnp.where(layer > 0, below_in[c, at, :], 0.0)
                if k < top:
                    beside = beside + guess[c, k + 1, at, :]
                else:
                    beside = beside + jnp.where(layer < n_layer - 1, above_in[c, at, :], 0.0)
                out[c] = rhs[c, k, at, :] - (out[c] - couple[c, k, at, :] * beside)
            return out

        f = None
        for k in range(DEPTH):
            res = residual(k)
            f = vec(load(pivot, k), res if k == 0 else sub(res, vec(load(lower, k), f)))
            for c in range(3):
                forward[c, k] = f[c]
        s, well_const = f, None
        for k in reversed(range(DEPTH)):
            if k < top:
                s = sub([forward[c, k] for c in range(3)], vec(load(pivot, k), vec(load(upper, k), s)))
            more = vec(load(well, k), s)
            well_const = more if k == top else add(well_const, more)
            for c in range(3):
                trial_out[c, k, at, :] = s[c]
        for c in range(3):
            put(send, h, SOURCE + c, f[c], s[c])
            total = jnp.sum(well_const[c], axis=1, keepdims=True)
            well_sums = well_sums + jnp.where(lane == c * ROWS + 8 * h + row, total, 0.0)
    well_out[...] = jnp.broadcast_to(jnp.sum(well_sums, axis=0, keepdims=True), (8, LANES))


def chain_kernel(peers, got, well_sums, send, step_ref, base_ref, inflow_ref):
    layer = lax.axis_index("layer")
    is_left = iota((peers, LANES), 1) < HALF

    def take(place, count):
        return [got[pl.ds(place + e, peers, PACK), :] for e in range(count)]

    def chain(base, order):
        for c in range(3):
            base_ref[c] = base[c]
        x = [jnp.zeros((1, LANES), jnp.float32)] * 3
        for d in order:
            at = slice(d, d + 1)
            for c in range(3):
                inflow_ref[c, at, :] = x[c]
            x = add([base_ref[c, at, :] for c in range(3)], vec([step_ref[e, at, :] for e in range(9)], x))
        return [inflow_ref[c] for c in range(3)]

    for e, step in enumerate(take(STEP, 9)):
        step_ref[e] = step
    source = take(SOURCE, 3)
    mixed = take(MIXED, 9)
    down = chain(source, range(peers))
    up_base = add(source, vec(mixed, [pltpu.roll(x, HALF, 1) for x in down]))
    up = chain(up_base, reversed(range(peers)))
    both = [jnp.where(is_left, a, b) for a, b in zip(down, up)]
    coef = [jnp.where(is_left, a, b) for a, b in zip(mixed, take(WELL, 9))]
    parts = vec(coef, both)
    mine = well_sums[0:1, :]
    one = iota((1, LANES), 1)
    for c in range(3):
        total = jnp.sum(jnp.sum(parts[c], axis=0, keepdims=True), axis=1, keepdims=True)
        mine = mine + jnp.where(one == c * ROWS + layer // 2, total, 0.0)
        send[pl.ds(c, peers, BACK), :] = both[c]
    send[pl.ds(3, peers, BACK), :] = jnp.broadcast_to(mine, (peers, LANES))
    for place in range(4, BACK):
        send[pl.ds(place, peers, BACK), :] = jnp.zeros((peers, LANES), jnp.float32)


def solved_kernel(areas, peers, got, cross, state, trial, solved, sums):
    is_left = iota((ROWS, LANES), 1) < HALF
    u, w = [], []
    for c in range(3):
        low_cols = got[pl.ds(c, ROWS, 2 * BACK), :]
        high_cols = got[pl.ds(BACK + c, ROWS, 2 * BACK), :]
        u.append(jnp.where(is_left, low_cols, pltpu.roll(high_cols, HALF, 1)))
        w.append(jnp.where(is_left, pltpu.roll(low_cols, HALF, 1), high_cols))
    total = jnp.sum(got[pl.ds(3, peers, BACK), :], axis=0, keepdims=True)
    sums[...] = jnp.broadcast_to(total, (8 * areas, LANES))
    for k in range(DEPTH):
        part = add(vec([cross[e, k] for e in range(9)], u), vec([state[e, k] for e in range(9)], w))
        for c in range(3):
            solved[c, k] = trial[c, k] + part[c]


def wells_kernel(areas, sums, same, block, solved, well, out):
    gathered = jnp.zeros((ROWS, LANES), jnp.float32)
    for a in range(areas):
        gathered = gathered + jnp.where(same[a] > 0.0, sums[8 * a : 8 * a + 1, :], 0.0)
    wide = iota((ROWS, LANES), 1)
    totals = [
        jnp.sum(
            jnp.where((wide >= c * ROWS) & (wide < (c + 1) * ROWS), gathered, 0.0),
            axis=1,
            keepdims=True,
        )
        for c in range(3)
    ]
    rate = vec([block[e] for e in range(9)], totals)
    for k in range(DEPTH):
        for c in range(3):
            out[c, k] = solved[c, k] - (
                well[c, k] * rate[0] + well[3 + c, k] * rate[1] + well[6 + c, k] * rate[2]
            )


def f32(*shape):
    return jax.ShapeDtypeStruct(shape, jnp.float32)


VMEM = pl.BlockSpec(memory_space=pltpu.VMEM)
SMEM = pl.BlockSpec(memory_space=pltpu.SMEM)
LONG = pl.CostEstimate(flops=20_000_000, bytes_accessed=8_000_000, transcendentals=0)
FIRST = pl.CostEstimate(flops=20_000_000_000, bytes_accessed=80_000_000, transcendentals=0)


def call(kernel, out_shape, in_specs, scratch=(), cost=None, aliases=None):
    return pl.pallas_call(
        kernel,
        out_shape=out_shape,
        in_specs=in_specs,
        out_specs=jax.tree.map(lambda _: VMEM, out_shape),
        scratch_shapes=scratch,
        cost_estimate=cost,
        input_output_aliases=aliases or {},
        compiler_params=pltpu.CompilerParams(vmem_limit_bytes=32 * 1024 * 1024),
    )


def moved(value, axis, by):
    count = lax.axis_size(axis)
    return lax.ppermute(value, axis, [(i, (i + by) % count) for i in range(count)])


def exchanged(value, axes):
    return lax.all_to_all(value, axes, split_axis=0, concat_axis=0, tiled=True)


def local(rhs, guess, diag, couple, pivot, lower, upper, well, inverse, tiles, counts):
    peers = lax.axis_size("layer")
    areas = lax.axis_size(AREA)
    cells = (DEPTH, ROWS, LANES)
    x_face, right_face, left_face, top_face, bottom_face = call(
        edges_kernel,
        (
            f32(3 * DEPTH, LANES), f32(ROWS, LANES), f32(ROWS, LANES),
            f32(3, ROWS, LANES), f32(3, ROWS, LANES),
        ),
        [VMEM],
        cost=FIRST,
    )(guess)
    below_in = moved(top_face, "layer", 1)
    above_in = moved(bottom_face, "layer", -1)
    right_in = moved(right_face, "column", 1)
    left_in = moved(left_face, "column", -1)
    x_in = moved(x_face, "region", 1)
    nine, three = f32(9, *cells), f32(3, *cells)
    send, cross, state, same, block = call(
        lambda *refs: maps_kernel(areas, tiles.shape[0], counts.shape[0], *refs),
        (f32(peers * PACK, LANES), nine, nine, f32(areas, ROWS, LANES), f32(9, ROWS, LANES)),
        [SMEM] * 3 + [VMEM] * 4,
        [pltpu.VMEM((9, DEPTH, 8, LANES), jnp.float32)],
        cost=LONG,
    )(tiles, counts, inverse, pivot, lower, upper, well)
    send, trial, well_sums = call(
        trial_kernel,
        (f32(peers * PACK, LANES), three, f32(8, LANES)),
        [VMEM] * 14,
        [pltpu.VMEM((3, DEPTH, 8, LANES), jnp.float32)],
        aliases={13: 0},
    )(x_in, right_in, left_in, below_in, above_in, rhs, guess, diag, couple, pivot, lower, upper, well, send)
    got = exchanged(send.reshape(peers, PACK, LANES), "layer").reshape(peers * PACK, LANES)
    back = call(
        lambda *refs: chain_kernel(peers, *refs),
        f32(peers * BACK, LANES),
        [VMEM] * 2,
        [
            pltpu.VMEM((9, peers, LANES), jnp.float32),
            pltpu.VMEM((3, peers, LANES), jnp.float32),
            pltpu.VMEM((3, peers, LANES), jnp.float32),
        ],
    )(got, well_sums)
    got = exchanged(back.reshape(peers, BACK, LANES), "layer").reshape(peers * BACK, LANES)
    solved, sums = call(
        lambda *refs: solved_kernel(areas, peers, *refs), (three, f32(8 * areas, LANES)), [VMEM] * 4
    )(got, cross, state, trial)
    sums = exchanged(sums.reshape(areas, 8, LANES), AREA).reshape(8 * areas, LANES)
    return call(lambda *refs: wells_kernel(areas, *refs), three, [VMEM] * 5)(
        sums, same, block, solved, well
    )


def solution(mesh):
    cells = P(None, "layer", "region", "column")
    return jax.shard_map(
        local,
        mesh=mesh,
        in_specs=(cells,) * 8 + (P(),) * 3,
        out_specs=cells,
        check_vma=False,
    )
```

```python
import jax
import jax.numpy as jnp
from jax import lax
from jax.experimental import pallas as pl
from jax.experimental.pallas import tpu as pltpu
from jax.sharding import PartitionSpec as P

AREA = ("region", "column")
DEPTH, ROWS, LANES = 8, 16, 128
HALF = LANES // 2
PACK = 26
BACK = 4

STEP, MIXED, WELL, SOURCE = 0, 9, 18, 23


def mat(a, b):
    return [
        a[3 * i] * b[m] + a[3 * i + 1] * b[3 + m] + a[3 * i + 2] * b[6 + m]
        for i in range(3)
        for m in range(3)
    ]


def vec(a, x):
    return [a[3 * i] * x[0] + a[3 * i + 1] * x[1] + a[3 * i + 2] * x[2] for i in range(3)]


def neg(a):
    return [-entry for entry in a]


def add(a, b):
    return [x + y for x, y in zip(a, b)]


def sub(a, b):
    return [x - y for x, y in zip(a, b)]


def iota(shape, axis):
    return lax.broadcasted_iota(jnp.int32, shape, axis)


def edges_kernel(guess, x_out, right_out, left_out, top_out, bottom_out):
    region = lax.axis_index("region")
    lane = iota((ROWS, LANES), 1)
    right = jnp.zeros((ROWS, LANES), jnp.float32)
    left = jnp.zeros((ROWS, LANES), jnp.float32)
    for c in range(3):
        for k in range(DEPTH):
            place = c * DEPTH + k
            block = guess[c, k]
            right = jnp.where(lane == place, pltpu.roll(block, (place + 1) % LANES, 1), right)
            left = jnp.where(lane == place, pltpu.roll(block, place, 1) if place else block, left)
            x_out[place : place + 1, :] = jnp.where(
                region == 0, guess[c, k, ROWS - 1 :, :], guess[c, k, :1, :]
            )
        top_out[c] = guess[c, DEPTH - 1]
        bottom_out[c] = guess[c, 0]
    right_out[...] = right
    left_out[...] = left


def put(send, h, place, left, right):
    is_left = iota((8, LANES), 1) < HALF
    low_cols = jnp.where(is_left, left, pltpu.roll(right, HALF, 1))
    high_cols = jnp.where(is_left, pltpu.roll(left, HALF, 1), right)
    send[pl.ds(16 * h * PACK + place, 8, 2 * PACK), :] = low_cols
    send[pl.ds((16 * h + 1) * PACK + place, 8, 2 * PACK), :] = high_cols


def well_masks(areas, nperf, nwell, tiles, counts, inverse, same_out, block_out):
    me = lax.axis_index("region") * lax.axis_size("column") + lax.axis_index("column")
    tile_all = iota((areas, LANES), 0) * ROWS + iota((areas, LANES), 1) % ROWS
    tile_own = me * ROWS + iota((ROWS, LANES), 0)
    place_all = jnp.full((areas, LANES), -1, jnp.int32)
    place_own = jnp.full((ROWS, LANES), -1, jnp.int32)
    for p in range(nperf):
        place_all = jnp.where(tile_all == tiles[p], p, place_all)
        place_own = jnp.where(tile_own == tiles[p], p, place_own)
    well_all = jnp.where(place_all < 0, -1, 0)
    well_own = jnp.where(place_own < 0, -2, 0)
    end = 0
    for w in range(nwell):
        end = end + counts[w]
        well_all = well_all + (place_all >= end).astype(jnp.int32)
        well_own = well_own + (place_own >= end).astype(jnp.int32)
    for a in range(areas):
        same_out[a] = (well_own == well_all[a : a + 1, :]).astype(jnp.float32)
    for e in range(9):
        entry = jnp.zeros((ROWS, LANES), jnp.float32)
        for w in range(nwell):
            entry = jnp.where(well_own == w, inverse[e, w], entry)
        block_out[e] = entry


def maps_kernel(
    areas, nperf, nwell,
    tiles, counts, inverse, pivot, lower, upper, well,
    send, cross_out, state_out, same_out, block_out, states,
):
    well_masks(areas, nperf, nwell, tiles, counts, inverse, same_out, block_out)
    top = DEPTH - 1
    for h in range(2):
        at = slice(8 * h, 8 * h + 8)

        def load(ref, k):
            return [ref[c, k, at, :] for c in range(9)]

        state = None
        for k in range(DEPTH):
            low = load(lower, k)
            state = neg(mat(load(pivot, k), low if k == 0 else mat(low, state)))
            for c in range(9):
                states[c, k] = state[c]
        down = state
        cross = state
        well_state, well_cross = None, None
        for k in reversed(range(DEPTH)):
            both = mat(load(pivot, k), load(upper, k))
            if k == top:
                state = neg(both)
            else:
                cross = sub([states[c, k] for c in range(9)], mat(both, cross))
                state = neg(mat(both, state))
            coef = load(well, k)
            more_state, more_cross = mat(coef, state), mat(coef, cross)
            well_state = more_state if k == top else add(well_state, more_state)
            well_cross = more_cross if k == top else add(well_cross, more_cross)
            for c in range(9):
                cross_out[c, k, at, :] = cross[c]
                state_out[c, k, at, :] = state[c]
        zero = jnp.zeros((8, LANES), jnp.float32)
        for e in range(9):
            put(send, h, STEP + e, down[e], state[e])
            put(send, h, MIXED + e, well_cross[e], cross[e])
        for e in range(5):
            put(send, h, WELL + e, well_state[e], well_state[5 + e] if e < 4 else zero)


def trial_kernel(
    x_in, right_in, left_in, below_in, above_in, rhs, guess, diag, couple, pivot, lower, upper, well, sent,
    send, trial_out, well_out, forward,
):
    region = lax.axis_index("region")
    column = lax.axis_index("column")
    layer = lax.axis_index("layer")
    n_column = lax.axis_size("column")
    n_layer = lax.axis_size("layer")
    lane = iota((8, LANES), 1)
    row = iota((8, LANES), 0)
    top = DEPTH - 1
    well_sums = jnp.zeros((8, LANES), jnp.float32)
    for h in range(2):
        at = slice(8 * h, 8 * h + 8)

        def load(ref, k, count=9):
            return [ref[c, k, at, :] for c in range(count)]

        edge_right = jnp.where(column > 0, right_in[at, :], 0.0)
        edge_left = jnp.where(column < n_column - 1, left_in[at, :], 0.0)

        def residual(k):
            mid = load(guess, k, 3)
            out = vec(load(diag, k), mid)
            for c in range(3):
                g = mid[c]
                place = c * DEPTH + k
                x_row = x_in[place : place + 1, :]
                if h == 0:
                    outer = jnp.where(region > 0, x_row, 0.0)
                    below = jnp.where(row == 0, outer, pltpu.roll(g, 1, 0))
                    above = guess[c, k, 1:9, :]
                else:
                    outer = jnp.where(region == 0, x_row, 0.0)
                    below = guess[c, k, 7:15, :]
                    above = jnp.where(row == 7, outer, pltpu.roll(g, 7, 0))
                first = pltpu.roll(edge_right, LANES - place, 1) if place else edge_right
                before = jnp.where(lane == 0, first, pltpu.roll(g, 1, 1))
                last = pltpu.roll(edge_left, LANES - 1 - place, 1)
                after = jnp.where(lane == LANES - 1, last, pltpu.roll(g, LANES - 1, 1))
                beside = below + above + before + after
                if k > 0:
                    beside = beside + guess[c, k - 1, at, :]
                else:
                    beside = beside + jnp.where(layer > 0, below_in[c, at, :], 0.0)
                if k < top:
                    beside = beside + guess[c, k + 1, at, :]
                else:
                    beside = beside + jnp.where(layer < n_layer - 1, above_in[c, at, :], 0.0)
                out[c] = rhs[c, k, at, :] - (out[c] - couple[c, k, at, :] * beside)
            return out

        f = None
        for k in range(DEPTH):
            res = residual(k)
            f = vec(load(pivot, k), res if k == 0 else sub(res, vec(load(lower, k), f)))
            for c in range(3):
                forward[c, k] = f[c]
        s, well_const = f, None
        for k in reversed(range(DEPTH)):
            if k < top:
                s = sub([forward[c, k] for c in range(3)], vec(load(pivot, k), vec(load(upper, k), s)))
            more = vec(load(well, k), s)
            well_const = more if k == top else add(well_const, more)
            for c in range(3):
                trial_out[c, k, at, :] = s[c]
        for c in range(3):
            put(send, h, SOURCE + c, f[c], s[c])
            total = jnp.sum(well_const[c], axis=1, keepdims=True)
            well_sums = well_sums + jnp.where(lane == c * ROWS + 8 * h + row, total, 0.0)
    well_out[...] = jnp.broadcast_to(jnp.sum(well_sums, axis=0, keepdims=True), (8, LANES))


def chain_kernel(peers, got, well_sums, send, step_ref, base_ref, inflow_ref):
    layer = lax.axis_index("layer")
    is_left = iota((peers, LANES), 1) < HALF

    def take(place, count):
        return [got[pl.ds(place + e, peers, PACK), :] for e in range(count)]

    def chain(base, order):
        for c in range(3):
            base_ref[c] = base[c]
        x = [jnp.zeros((1, LANES), jnp.float32)] * 3
        for d in order:
            at = slice(d, d + 1)
            for c in range(3):
                inflow_ref[c, at, :] = x[c]
            x = add([base_ref[c, at, :] for c in range(3)], vec([step_ref[e, at, :] for e in range(9)], x))
        return [inflow_ref[c] for c in range(3)]

    for e, step in enumerate(take(STEP, 9)):
        step_ref[e] = step
    source = take(SOURCE, 3)
    mixed = take(MIXED, 9)
    down = chain(source, range(peers))
    up_base = add(source, vec(mixed, [pltpu.roll(x, HALF, 1) for x in down]))
    up = chain(up_base, reversed(range(peers)))
    both = [jnp.where(is_left, a, b) for a, b in zip(down, up)]
    packed = take(WELL, 5)
    well_state = [pltpu.roll(x, HALF, 1) for x in packed] + packed[:4]
    coef = [jnp.where(is_left, a, b) for a, b in zip(mixed, well_state)]
    parts = vec(coef, both)
    mine = well_sums[0:1, :]
    one = iota((1, LANES), 1)
    for c in range(3):
        total = jnp.sum(jnp.sum(parts[c], axis=0, keepdims=True), axis=1, keepdims=True)
        mine = mine + jnp.where(one == c * ROWS + layer // 2, total, 0.0)
        send[pl.ds(c, peers, BACK), :] = both[c]
    send[pl.ds(3, peers, BACK), :] = jnp.broadcast_to(mine, (peers, LANES))
    for place in range(4, BACK):
        send[pl.ds(place, peers, BACK), :] = jnp.zeros((peers, LANES), jnp.float32)


def solved_kernel(areas, peers, got, cross, state, trial, solved, sums):
    is_left = iota((ROWS, LANES), 1) < HALF
    u, w = [], []
    for c in range(3):
        low_cols = got[pl.ds(c, ROWS, 2 * BACK), :]
        high_cols = got[pl.ds(BACK + c, ROWS, 2 * BACK), :]
        u.append(jnp.where(is_left, low_cols, pltpu.roll(high_cols, HALF, 1)))
        w.append(jnp.where(is_left, pltpu.roll(low_cols, HALF, 1), high_cols))
    total = jnp.sum(got[pl.ds(3, peers, BACK), :], axis=0, keepdims=True)
    sums[...] = jnp.broadcast_to(total, (8 * areas, LANES))
    for k in range(DEPTH):
        part = add(vec([cross[e, k] for e in range(9)], u), vec([state[e, k] for e in range(9)], w))
        for c in range(3):
            solved[c, k] = trial[c, k] + part[c]


def wells_kernel(areas, sums, same, block, solved, well, out):
    gathered = jnp.zeros((ROWS, LANES), jnp.float32)
    for a in range(areas):
        gathered = gathered + jnp.where(same[a] > 0.0, sums[8 * a : 8 * a + 1, :], 0.0)
    wide = iota((ROWS, LANES), 1)
    totals = [
        jnp.sum(
            jnp.where((wide >= c * ROWS) & (wide < (c + 1) * ROWS), gathered, 0.0),
            axis=1,
            keepdims=True,
        )
        for c in range(3)
    ]
    rate = vec([block[e] for e in range(9)], totals)
    for k in range(DEPTH):
        for c in range(3):
            out[c, k] = solved[c, k] - (
                well[c, k] * rate[0] + well[3 + c, k] * rate[1] + well[6 + c, k] * rate[2]
            )


def f32(*shape):
    return jax.ShapeDtypeStruct(shape, jnp.float32)


VMEM = pl.BlockSpec(memory_space=pltpu.VMEM)
SMEM = pl.BlockSpec(memory_space=pltpu.SMEM)
LONG = pl.CostEstimate(flops=20_000_000, bytes_accessed=8_000_000, transcendentals=0)
FIRST = pl.CostEstimate(flops=20_000_000_000, bytes_accessed=80_000_000, transcendentals=0)


def call(kernel, out_shape, in_specs, scratch=(), cost=None, aliases=None):
    return pl.pallas_call(
        kernel,
        out_shape=out_shape,
        in_specs=in_specs,
        out_specs=jax.tree.map(lambda _: VMEM, out_shape),
        scratch_shapes=scratch,
        cost_estimate=cost,
        input_output_aliases=aliases or {},
        compiler_params=pltpu.CompilerParams(vmem_limit_bytes=32 * 1024 * 1024),
    )


def moved(value, axis, by):
    count = lax.axis_size(axis)
    return lax.ppermute(value, axis, [(i, (i + by) % count) for i in range(count)])


def exchanged(value, axes):
    return lax.all_to_all(value, axes, split_axis=0, concat_axis=0, tiled=True)


def local(rhs, guess, diag, couple, pivot, lower, upper, well, inverse, tiles, counts):
    peers = lax.axis_size("layer")
    areas = lax.axis_size(AREA)
    cells = (DEPTH, ROWS, LANES)
    x_face, right_face, left_face, top_face, bottom_face = call(
        edges_kernel,
        (
            f32(3 * DEPTH, LANES), f32(ROWS, LANES), f32(ROWS, LANES),
            f32(3, ROWS, LANES), f32(3, ROWS, LANES),
        ),
        [VMEM],
        cost=FIRST,
    )(guess)
    below_in = moved(top_face, "layer", 1)
    above_in = moved(bottom_face, "layer", -1)
    right_in = moved(right_face, "column", 1)
    left_in = moved(left_face, "column", -1)
    x_in = moved(x_face, "region", 1)
    nine, three = f32(9, *cells), f32(3, *cells)
    send, cross, state, same, block = call(
        lambda *refs: maps_kernel(areas, tiles.shape[0], counts.shape[0], *refs),
        (f32(peers * PACK, LANES), nine, nine, f32(areas, ROWS, LANES), f32(9, ROWS, LANES)),
        [SMEM] * 3 + [VMEM] * 4,
        [pltpu.VMEM((9, DEPTH, 8, LANES), jnp.float32)],
        cost=LONG,
    )(tiles, counts, inverse, pivot, lower, upper, well)
    send, trial, well_sums = call(
        trial_kernel,
        (f32(peers * PACK, LANES), three, f32(8, LANES)),
        [VMEM] * 14,
        [pltpu.VMEM((3, DEPTH, 8, LANES), jnp.float32)],
        aliases={13: 0},
    )(x_in, right_in, left_in, below_in, above_in, rhs, guess, diag, couple, pivot, lower, upper, well, send)
    got = exchanged(send.reshape(peers, PACK, 1, LANES), "layer").reshape(peers * PACK, LANES)
    back = call(
        lambda *refs: chain_kernel(peers, *refs),
        f32(peers * BACK, LANES),
        [VMEM] * 2,
        [
            pltpu.VMEM((9, peers, LANES), jnp.float32),
            pltpu.VMEM((3, peers, LANES), jnp.float32),
            pltpu.VMEM((3, peers, LANES), jnp.float32),
        ],
    )(got, well_sums)
    got = exchanged(back.reshape(peers, BACK, 1, LANES), "layer").reshape(peers * BACK, LANES)
    solved, sums = call(
        lambda *refs: solved_kernel(areas, peers, *refs), (three, f32(8 * areas, LANES)), [VMEM] * 4
    )(got, cross, state, trial)
    sums = exchanged(sums.reshape(areas, 8, LANES), AREA).reshape(8 * areas, LANES)
    return call(lambda *refs: wells_kernel(areas, *refs), three, [VMEM] * 5)(
        sums, same, block, solved, well
    )


def solution(mesh):
    cells = P(None, "layer", "region", "column")
    return jax.shard_map(
        local,
        mesh=mesh,
        in_specs=(cells,) * 8 + (P(),) * 3,
        out_specs=cells,
        check_vma=False,
    )
```

```python
import jax
import jax.numpy as jnp
from jax import lax
from jax.experimental import pallas as pl
from jax.experimental.pallas import tpu as pltpu
from jax.sharding import PartitionSpec as P

AREA = ("region", "column")
DEPTH, ROWS, LANES = 8, 16, 128
HALF = LANES // 2
BLOCK = 16
GROUPS, ACROSS = 4, 8
PACK = 20
BACK = 4

TRIAL, WELLS = 3, 4


def mat(a, b):
    return [
        a[3 * i] * b[m] + a[3 * i + 1] * b[3 + m] + a[3 * i + 2] * b[6 + m]
        for i in range(3)
        for m in range(3)
    ]


def vec(a, x):
    return [a[3 * i] * x[0] + a[3 * i + 1] * x[1] + a[3 * i + 2] * x[2] for i in range(3)]


def neg(a):
    return [-entry for entry in a]


def add(a, b):
    return [x + y for x, y in zip(a, b)]


def sub(a, b):
    return [x - y for x, y in zip(a, b)]


def iota(shape, axis):
    return lax.broadcasted_iota(jnp.int32, shape, axis)


def edges_kernel(guess, x_out, right_out, left_out, top_out, bottom_out):
    region = lax.axis_index("region")
    lane = iota((ROWS, LANES), 1)
    right = jnp.zeros((ROWS, LANES), jnp.float32)
    left = jnp.zeros((ROWS, LANES), jnp.float32)
    for c in range(3):
        for k in range(DEPTH):
            place = c * DEPTH + k
            block = guess[c, k]
            right = jnp.where(lane == place, pltpu.roll(block, (place + 1) % LANES, 1), right)
            left = jnp.where(lane == place, pltpu.roll(block, place, 1) if place else block, left)
            x_out[place : place + 1, :] = jnp.where(
                region == 0, guess[c, k, ROWS - 1 :, :], guess[c, k, :1, :]
            )
        top_out[c] = guess[c, DEPTH - 1]
        bottom_out[c] = guess[c, 0]
    right_out[...] = right
    left_out[...] = left


def swapped(parts, steps):
    parts = list(parts)
    for step in steps:
        block = iota(parts[0].shape, 1) // BLOCK
        low = (block & step) == 0
        for i in range(len(parts)):
            if i & step == 0:
                a, b = parts[i], parts[i + step]
                parts[i] = jnp.where(low, a, pltpu.roll(b, BLOCK * step, 1))
                parts[i + step] = jnp.where(low, pltpu.roll(a, LANES - BLOCK * step, 1), b)
    return parts


def placed(low, high, index):
    inner = index & 7
    return jnp.where(
        index < 8,
        jnp.take_along_axis(low, inner, axis=0, mode="promise_in_bounds"),
        jnp.take_along_axis(high, inner, axis=0, mode="promise_in_bounds"),
    )


def put(send, h, m, parts):
    for e, part in enumerate(swapped(parts, (1, 2, 4))):
        for half in range(2):
            at = (ACROSS * (2 * h + half) + e) * PACK + 4 * m
            send[at : at + 4, :] = part[4 * half : 4 * half + 4, :]


def lane_sum(x):
    return jnp.sum(x, axis=1, keepdims=True)


def row_order(flag_lane, flag_row, order_out, place_out, group_out):
    row = iota((ROWS, LANES), 0)
    lane = iota((ROWS, LANES), 1)
    inner = lane % ROWS

    def place_of(flag, rank, number):
        free = number - rank
        return jnp.where(flag > 0.0, 4 * rank, free + 1 + ((free * 11) >> 5))

    rank_row = lane_sum(jnp.where((lane < ROWS) & (lane < row), flag_lane, 0.0))
    rank_lane = jnp.sum(jnp.where(row < inner, flag_row, 0.0), axis=0, keepdims=True)
    rank_row = jnp.broadcast_to(rank_row, (ROWS, LANES)).astype(jnp.int32)
    rank_lane = jnp.broadcast_to(rank_lane, (ROWS, LANES)).astype(jnp.int32)
    place_out[...] = place_of(flag_row, rank_row, row)
    at_lane = place_of(flag_lane, rank_lane, inner)
    number = jnp.where(lane < ROWS, lane, 0).astype(jnp.float32)
    for out, wanted in ((order_out, row), (group_out, row & 12)):
        found = lane_sum(jnp.where(at_lane == wanted, number, 0.0))
        out[...] = jnp.broadcast_to(found, (ROWS, LANES)).astype(jnp.int32)


def well_masks(areas, nperf, nwell, tiles, counts, inverse, same_out, block_out, order_out, place_out, group_out):
    me = lax.axis_index("region") * lax.axis_size("column") + lax.axis_index("column")
    tile_all = iota((areas, LANES), 0) * ROWS + iota((areas, LANES), 1) % ROWS
    tile_own = me * ROWS + iota((ROWS, LANES), 0)
    place_all = jnp.full((areas, LANES), -1, jnp.int32)
    place_own = jnp.full((ROWS, LANES), -1, jnp.int32)
    for p in range(nperf):
        place_all = jnp.where(tile_all == tiles[p], p, place_all)
        place_own = jnp.where(tile_own == tiles[p], p, place_own)
    own_area = (iota((areas, LANES), 0) == me) & (place_all >= 0)
    flag_lane = jnp.sum(jnp.where(own_area, 1.0, 0.0), axis=0, keepdims=True)
    flag_lane = jnp.broadcast_to(flag_lane, (ROWS, LANES))
    row_order(flag_lane, jnp.where(place_own >= 0, 1.0, 0.0), order_out, place_out, group_out)
    well_all = jnp.where(place_all < 0, -1, 0)
    well_own = jnp.where(place_own < 0, -2, 0)
    end = 0
    for w in range(nwell):
        end = end + counts[w]
        well_all = well_all + (place_all >= end).astype(jnp.int32)
        well_own = well_own + (place_own >= end).astype(jnp.int32)
    for a in range(areas):
        same_out[a] = (well_own == well_all[a : a + 1, :]).astype(jnp.float32)
    for e in range(9):
        entry = jnp.zeros((ROWS, LANES), jnp.float32)
        for w in range(nwell):
            entry = jnp.where(well_own == w, inverse[e, w], entry)
        block_out[e] = entry


def maps_kernel(
    areas, nperf, nwell,
    tiles, counts, inverse, pivot, lower, upper, well,
    send, cross_out, state_out, same_out, block_out, order, place_out, rest, states, maps, group,
):
    well_masks(
        areas, nperf, nwell, tiles, counts, inverse, same_out, block_out, order, place_out, group
    )
    top = DEPTH - 1
    for h in range(2):
        at = slice(8 * h, 8 * h + 8)

        def load(ref, k):
            return [ref[c, k, at, :] for c in range(9)]

        state = None
        for k in range(DEPTH):
            low = load(lower, k)
            state = neg(mat(load(pivot, k), low if k == 0 else mat(low, state)))
            for c in range(9):
                states[c, k] = state[c]
        down = state
        cross = state
        well_state, well_cross = None, None
        for k in reversed(range(DEPTH)):
            both = mat(load(pivot, k), load(upper, k))
            if k == top:
                state = neg(both)
            else:
                cross = sub([states[c, k] for c in range(9)], mat(both, cross))
                state = neg(mat(both, state))
            coef = load(well, k)
            more_state, more_cross = mat(coef, state), mat(coef, cross)
            well_state = more_state if k == top else add(well_state, more_state)
            well_cross = more_cross if k == top else add(well_cross, more_cross)
            for c in range(9):
                cross_out[c, k, at, :] = cross[c]
                state_out[c, k, at, :] = state[c]
        zero = jnp.zeros((8, LANES), jnp.float32)
        for e in range(9):
            maps[e, at, :] = down[e]
            maps[9 + e, at, :] = state[e]
            maps[18 + e, at, :] = cross[e]
            maps[27 + e, at, :] = well_cross[e]
            maps[36 + e, at, :] = well_state[e]
    for h in range(2):
        at = slice(8 * h, 8 * h + 8)

        def take(e, index):
            return placed(maps[e, 0:8, :], maps[e, 8:16, :], index[at, :])

        down = [take(e, order) for e in range(9)]
        state = [take(9 + e, order) for e in range(9)]
        cross = [take(18 + e, order) for e in range(9)]
        wells = [take(27 + e, group) for e in range(18)]
        put(send, h, 0, down[:4] + state[:4])
        put(send, h, 1, down[4:8] + state[4:8])
        put(send, h, 2, [down[8], cross[0], cross[2], cross[4], state[8], cross[1], cross[3], cross[5]])
        rest[0, at, :] = cross[6]
        rest[1, at, :] = cross[7]
        j = iota((8, LANES), 0) & 3
        behind = []
        for b in range(7):
            value = jnp.where(j == 0, wells[b], wells[7 + b])
            behind.append(value if b > 3 else jnp.where(j == 2, wells[14 + b], value))
        put(send, h, WELLS, [cross[8]] + behind)


def trial_kernel(
    x_in, right_in, left_in, below_in, above_in, rhs, guess, diag, couple, pivot, lower, upper, well, order, rest, sent,
    send, trial_out, well_out, forward, ends,
):
    region = lax.axis_index("region")
    column = lax.axis_index("column")
    layer = lax.axis_index("layer")
    n_column = lax.axis_size("column")
    n_layer = lax.axis_size("layer")
    lane = iota((8, LANES), 1)
    row = iota((8, LANES), 0)
    top = DEPTH - 1
    well_sums = jnp.zeros((8, LANES), jnp.float32)
    for h in range(2):
        at = slice(8 * h, 8 * h + 8)

        def load(ref, k, count=9):
            return [ref[c, k, at, :] for c in range(count)]

        edge_right = jnp.where(column > 0, right_in[at, :], 0.0)
        edge_left = jnp.where(column < n_column - 1, left_in[at, :], 0.0)

        def residual(k):
            mid = load(guess, k, 3)
            out = vec(load(diag, k), mid)
            for c in range(3):
                g = mid[c]
                place = c * DEPTH + k
                x_row = x_in[place : place + 1, :]
                if h == 0:
                    outer = jnp.where(region > 0, x_row, 0.0)
                    below = jnp.where(row == 0, outer, pltpu.roll(g, 1, 0))
                    above = guess[c, k, 1:9, :]
                else:
                    outer = jnp.where(region == 0, x_row, 0.0)
                    below = guess[c, k, 7:15, :]
                    above = jnp.where(row == 7, outer, pltpu.roll(g, 7, 0))
                first = pltpu.roll(edge_right, LANES - place, 1) if place else edge_right
                before = jnp.where(lane == 0, first, pltpu.roll(g, 1, 1))
                last = pltpu.roll(edge_left, LANES - 1 - place, 1)
                after = jnp.where(lane == LANES - 1, last, pltpu.roll(g, LANES - 1, 1))
                beside = below + above + before + after
                if k > 0:
                    beside = beside + guess[c, k - 1, at, :]
                else:
                    beside = beside + jnp.where(layer > 0, below_in[c, at, :], 0.0)
                if k < top:
                    beside = beside + guess[c, k + 1, at, :]
                else:
                    beside = beside + jnp.where(layer < n_layer - 1, above_in[c, at, :], 0.0)
                out[c] = rhs[c, k, at, :] - (out[c] - couple[c, k, at, :] * beside)
            return out

        f = None
        for k in range(DEPTH):
            res = residual(k)
            f = vec(load(pivot, k), res if k == 0 else sub(res, vec(load(lower, k), f)))
            for c in range(3):
                forward[c, k] = f[c]
        s, well_const = f, None
        for k in reversed(range(DEPTH)):
            if k < top:
                s = sub([forward[c, k] for c in range(3)], vec(load(pivot, k), vec(load(upper, k), s)))
            more = vec(load(well, k), s)
            well_const = more if k == top else add(well_const, more)
            for c in range(3):
                trial_out[c, k, at, :] = s[c]
        for c in range(3):
            ends[c, at, :] = f[c]
            ends[3 + c, at, :] = s[c]
            total = jnp.sum(well_const[c], axis=1, keepdims=True)
            well_sums = well_sums + jnp.where(lane == c * ROWS + 8 * h + row, total, 0.0)
    for h in range(2):
        at = slice(8 * h, 8 * h + 8)
        source = [placed(ends[c, 0:8, :], ends[c, 8:16, :], order[at, :]) for c in range(6)]
        put(send, h, TRIAL, source[:3] + [rest[0, at, :]] + source[3:] + [rest[1, at, :]])
    well_out[...] = jnp.broadcast_to(jnp.sum(well_sums, axis=0, keepdims=True), (8, LANES))


def chain_kernel(peers, got, well_sums, order_in, send, step_ref, base_ref, inflow_ref):
    layer = lax.axis_index("layer")
    is_left = iota((peers, LANES), 1) < HALF

    def rows(m):
        return [got[pl.ds(4 * m + j, peers, PACK), :] for j in range(4)]

    def turn(x):
        return pltpu.roll(x, HALF, 1)

    def chain(base, order):
        for c in range(3):
            base_ref[c] = base[c]
        x = [jnp.zeros((1, LANES), jnp.float32)] * 3
        for d in order:
            at = slice(d, d + 1)
            for c in range(3):
                inflow_ref[c, at, :] = x[c]
            x = add([base_ref[c, at, :] for c in range(3)], vec([step_ref[e, at, :] for e in range(9)], x))
        return [inflow_ref[c] for c in range(3)]

    sets = [swapped(rows(m), (1, 2)) for m in range(4)]
    for e in range(9):
        step_ref[e] = sets[e // 4][e % 4]
    source = sets[TRIAL][:3]
    last = rows(WELLS)
    mixed = []
    for pair in sets[2][1:] + [sets[TRIAL][3], swapped(last, (1, 2))[0]]:
        mixed += [turn(pair), pair]
    down = chain(source, range(peers))
    up_base = add(source, vec(mixed[:9], [turn(x) for x in down]))
    up = chain(up_base, reversed(range(peers)))
    both = [jnp.where(is_left, a, b) for a, b in zip(down, up)]
    block = iota((peers, LANES), 1) // BLOCK
    parts = []
    for j in range(3):
        factor = jnp.zeros((peers, LANES), jnp.float32)
        for b in range(7):
            w = 7 * j + b
            if w < 18:
                shift = BLOCK * (b + 1 - (0 if w < 9 else 4)) % LANES
                value = both[w % 3]
                factor = jnp.where(block == b + 1, pltpu.roll(value, shift, 1) if shift else value, factor)
        parts.append(jnp.sum(last[j] * factor, axis=0, keepdims=True))
    mine = well_sums[0:1, :]
    one = iota((1, LANES), 1)
    leader = order_in[pl.ds(4 * (layer // ACROSS), 1), :]
    for c in range(3):
        total = jnp.zeros((1, LANES), jnp.float32)
        for j in range(3):
            for b in range(7):
                w = 7 * j + b
                if w < 18 and (w % 9) // 3 == c:
                    total = total + jnp.where(one // BLOCK == b + 1, parts[j], 0.0)
        mine = mine + jnp.where(one == c * ROWS + leader, lane_sum(total), 0.0)
        send[pl.ds(c, peers, BACK), :] = both[c]
    send[pl.ds(3, peers, BACK), :] = jnp.broadcast_to(mine, (peers, LANES))


def solved_kernel(areas, peers, got, cross, state, trial, place_in, solved, sums, inflow):
    for c in range(3):
        parts = [got[pl.ds(e * BACK + c, GROUPS, ACROSS * BACK), :] for e in range(ACROSS)]
        for i, part in enumerate(swapped(parts, (1, 2, 4))):
            inflow[3 * (i // 4) + c, pl.ds(i % 4, GROUPS, 4), :] = part

    def rows_of(c):
        low, high = inflow[c, 0:8, :], inflow[c, 8:16, :]
        return jnp.concatenate(
            [placed(low, high, place_in[0:8, :]), placed(low, high, place_in[8:16, :])], axis=0
        )

    u = [rows_of(c) for c in range(3)]
    w = [rows_of(3 + c) for c in range(3)]
    total = jnp.sum(got[pl.ds(3, peers, BACK), :], axis=0, keepdims=True)
    sums[...] = jnp.broadcast_to(total, (8 * areas, LANES))
    for k in range(DEPTH):
        part = add(vec([cross[e, k] for e in range(9)], u), vec([state[e, k] for e in range(9)], w))
        for c in range(3):
            solved[c, k] = trial[c, k] + part[c]


def wells_kernel(areas, sums, same, block, solved, well, out):
    gathered = jnp.zeros((ROWS, LANES), jnp.float32)
    for a in range(areas):
        gathered = gathered + jnp.where(same[a] > 0.0, sums[8 * a : 8 * a + 1, :], 0.0)
    wide = iota((ROWS, LANES), 1)
    totals = [
        jnp.sum(
            jnp.where((wide >= c * ROWS) & (wide < (c + 1) * ROWS), gathered, 0.0),
            axis=1,
            keepdims=True,
        )
        for c in range(3)
    ]
    rate = vec([block[e] for e in range(9)], totals)
    for k in range(DEPTH):
        for c in range(3):
            out[c, k] = solved[c, k] - (
                well[c, k] * rate[0] + well[3 + c, k] * rate[1] + well[6 + c, k] * rate[2]
            )


def f32(*shape):
    return jax.ShapeDtypeStruct(shape, jnp.float32)


VMEM = pl.BlockSpec(memory_space=pltpu.VMEM)
SMEM = pl.BlockSpec(memory_space=pltpu.SMEM)
LONG = pl.CostEstimate(flops=20_000_000, bytes_accessed=8_000_000, transcendentals=0)
FIRST = pl.CostEstimate(flops=20_000_000_000, bytes_accessed=80_000_000, transcendentals=0)


def call(kernel, out_shape, in_specs, scratch=(), cost=None, aliases=None):
    return pl.pallas_call(
        kernel,
        out_shape=out_shape,
        in_specs=in_specs,
        out_specs=jax.tree.map(lambda _: VMEM, out_shape),
        scratch_shapes=scratch,
        cost_estimate=cost,
        input_output_aliases=aliases or {},
        compiler_params=pltpu.CompilerParams(vmem_limit_bytes=32 * 1024 * 1024),
    )


def moved(value, axis, by):
    count = lax.axis_size(axis)
    return lax.ppermute(value, axis, [(i, (i + by) % count) for i in range(count)])


def exchanged(value, axes):
    return lax.all_to_all(value, axes, split_axis=0, concat_axis=0, tiled=True)


def local(rhs, guess, diag, couple, pivot, lower, upper, well, inverse, tiles, counts):
    peers = lax.axis_size("layer")
    areas = lax.axis_size(AREA)
    cells = (DEPTH, ROWS, LANES)
    x_face, right_face, left_face, top_face, bottom_face = call(
        edges_kernel,
        (
            f32(3 * DEPTH, LANES), f32(ROWS, LANES), f32(ROWS, LANES),
            f32(3, ROWS, LANES), f32(3, ROWS, LANES),
        ),
        [VMEM],
        cost=FIRST,
    )(guess)
    below_in = moved(top_face, "layer", 1)
    above_in = moved(bottom_face, "layer", -1)
    right_in = moved(right_face, "column", 1)
    left_in = moved(left_face, "column", -1)
    x_in = moved(x_face, "region", 1)
    nine, three = f32(9, *cells), f32(3, *cells)
    index = jax.ShapeDtypeStruct((ROWS, LANES), jnp.int32)
    send, cross, state, same, block, order, place, rest = call(
        lambda *refs: maps_kernel(areas, tiles.shape[0], counts.shape[0], *refs),
        (
            f32(peers * PACK, LANES), nine, nine, f32(areas, ROWS, LANES), f32(9, ROWS, LANES),
            index, index, f32(2, ROWS, LANES),
        ),
        [SMEM] * 3 + [VMEM] * 4,
        [
            pltpu.VMEM((9, DEPTH, 8, LANES), jnp.float32),
            pltpu.VMEM((45, ROWS, LANES), jnp.float32),
            pltpu.VMEM((ROWS, LANES), jnp.int32),
        ],
        cost=LONG,
    )(tiles, counts, inverse, pivot, lower, upper, well)
    send, trial, well_sums = call(
        trial_kernel,
        (f32(peers * PACK, LANES), three, f32(8, LANES)),
        [VMEM] * 16,
        [pltpu.VMEM((3, DEPTH, 8, LANES), jnp.float32), pltpu.VMEM((6, ROWS, LANES), jnp.float32)],
        aliases={15: 0},
    )(x_in, right_in, left_in, below_in, above_in, rhs, guess, diag, couple, pivot, lower, upper, well, order, rest, send)
    got = exchanged(send.reshape(peers, PACK, 1, LANES), "layer").reshape(peers * PACK, LANES)
    back = call(
        lambda *refs: chain_kernel(peers, *refs),
        f32(peers * BACK, LANES),
        [VMEM] * 3,
        [
            pltpu.VMEM((9, peers, LANES), jnp.float32),
            pltpu.VMEM((3, peers, LANES), jnp.float32),
            pltpu.VMEM((3, peers, LANES), jnp.float32),
        ],
    )(got, well_sums, order)
    got = exchanged(back.reshape(peers, BACK, 1, LANES), "layer").reshape(peers * BACK, LANES)
    solved, sums = call(
        lambda *refs: solved_kernel(areas, peers, *refs), (three, f32(8 * areas, LANES)), [VMEM] * 5,
        [pltpu.VMEM((6, ROWS, LANES), jnp.float32)],
    )(got, cross, state, trial, place)
    sums = exchanged(sums.reshape(areas, 8, LANES), AREA).reshape(8 * areas, LANES)
    return call(lambda *refs: wells_kernel(areas, *refs), three, [VMEM] * 5)(
        sums, same, block, solved, well
    )


def solution(mesh):
    cells = P(None, "layer", "region", "column")
    return jax.shard_map(
        local,
        mesh=mesh,
        in_specs=(cells,) * 8 + (P(),) * 3,
        out_specs=cells,
        check_vma=False,
    )
```

```python
import jax
import jax.numpy as jnp
from jax import lax
from jax.experimental import pallas as pl
from jax.experimental.pallas import tpu as pltpu
from jax.sharding import PartitionSpec as P

AREA = ("region", "column")
DEPTH, ROWS, LANES = 8, 16, 128
HALF = LANES // 2
BLOCK = 16
GROUPS, ACROSS = 4, 8
PACK = 20
BACK = 4

TRIAL, WELLS = 3, 4


def mat(a, b):
    return [
        a[3 * i] * b[m] + a[3 * i + 1] * b[3 + m] + a[3 * i + 2] * b[6 + m]
        for i in range(3)
        for m in range(3)
    ]


def vec(a, x):
    return [a[3 * i] * x[0] + a[3 * i + 1] * x[1] + a[3 * i + 2] * x[2] for i in range(3)]


def neg(a):
    return [-entry for entry in a]


def add(a, b):
    return [x + y for x, y in zip(a, b)]


def sub(a, b):
    return [x - y for x, y in zip(a, b)]


def iota(shape, axis):
    return lax.broadcasted_iota(jnp.int32, shape, axis)


def edges_kernel(guess, x_out, right_out, left_out, top_out, bottom_out):
    region = lax.axis_index("region")
    lane = iota((ROWS, LANES), 1)
    right = jnp.zeros((ROWS, LANES), jnp.float32)
    left = jnp.zeros((ROWS, LANES), jnp.float32)
    for c in range(3):
        for k in range(DEPTH):
            place = c * DEPTH + k
            block = guess[c, k]
            right = jnp.where(lane == place, pltpu.roll(block, (place + 1) % LANES, 1), right)
            left = jnp.where(lane == place, pltpu.roll(block, place, 1) if place else block, left)
            x_out[place : place + 1, :] = jnp.where(
                region == 0, guess[c, k, ROWS - 1 :, :], guess[c, k, :1, :]
            )
        top_out[c] = guess[c, DEPTH - 1]
        bottom_out[c] = guess[c, 0]
    right_out[...] = right
    left_out[...] = left


def swapped(parts, steps):
    parts = list(parts)
    for step in steps:
        block = iota(parts[0].shape, 1) // BLOCK
        low = (block & step) == 0
        for i in range(len(parts)):
            if i & step == 0:
                a, b = parts[i], parts[i + step]
                parts[i] = jnp.where(low, a, pltpu.roll(b, BLOCK * step, 1))
                parts[i + step] = jnp.where(low, pltpu.roll(a, LANES - BLOCK * step, 1), b)
    return parts


def placed(low, high, index):
    inner = index & 7
    return jnp.where(
        index < 8,
        jnp.take_along_axis(low, inner, axis=0, mode="promise_in_bounds"),
        jnp.take_along_axis(high, inner, axis=0, mode="promise_in_bounds"),
    )


def put(send, h, m, parts):
    for e, part in enumerate(swapped(parts, (1, 2, 4))):
        for half in range(2):
            at = (ACROSS * (2 * h + half) + e) * PACK + 4 * m
            send[at : at + 4, :] = part[4 * half : 4 * half + 4, :]


def lane_sum(x):
    return jnp.sum(x, axis=1, keepdims=True)


def row_order(flag_lane, flag_row, order_out, place_out, group_out):
    row = iota((ROWS, LANES), 0)
    lane = iota((ROWS, LANES), 1)
    inner = lane % ROWS

    def place_of(flag, rank, number):
        free = number - rank
        return jnp.where(flag > 0.0, 4 * rank, free + 1 + ((free * 11) >> 5))

    rank_row = lane_sum(jnp.where((lane < ROWS) & (lane < row), flag_lane, 0.0))
    rank_lane = jnp.sum(jnp.where(row < inner, flag_row, 0.0), axis=0, keepdims=True)
    rank_row = jnp.broadcast_to(rank_row, (ROWS, LANES)).astype(jnp.int32)
    rank_lane = jnp.broadcast_to(rank_lane, (ROWS, LANES)).astype(jnp.int32)
    place_out[...] = place_of(flag_row, rank_row, row)
    at_lane = place_of(flag_lane, rank_lane, inner)
    number = jnp.where(lane < ROWS, lane, 0).astype(jnp.float32)
    for out, wanted in ((order_out, row), (group_out, row & 12)):
        found = lane_sum(jnp.where(at_lane == wanted, number, 0.0))
        out[...] = jnp.broadcast_to(found, (ROWS, LANES)).astype(jnp.int32)


def own_area():
    return lax.axis_index("region") * lax.axis_size("column") + lax.axis_index("column")


def tile_places(areas, nperf, tiles):
    tile_all = iota((areas, LANES), 0) * ROWS + iota((areas, LANES), 1) % ROWS
    tile_own = own_area() * ROWS + iota((ROWS, LANES), 0)
    place_all = jnp.full((areas, LANES), -1, jnp.int32)
    place_own = jnp.full((ROWS, LANES), -1, jnp.int32)
    for p in range(nperf):
        place_all = jnp.where(tile_all == tiles[p], p, place_all)
        place_own = jnp.where(tile_own == tiles[p], p, place_own)
    return place_all, place_own


def well_masks(areas, nperf, nwell, tiles, counts, inverse, same_out, block_out):
    place_all, place_own = tile_places(areas, nperf, tiles)
    well_all = jnp.where(place_all < 0, -1, 0)
    well_own = jnp.where(place_own < 0, -2, 0)
    end = 0
    for w in range(nwell):
        end = end + counts[w]
        well_all = well_all + (place_all >= end).astype(jnp.int32)
        well_own = well_own + (place_own >= end).astype(jnp.int32)
    for a in range(areas):
        same_out[a] = (well_own == well_all[a : a + 1, :]).astype(jnp.float32)
    for e in range(9):
        entry = jnp.zeros((ROWS, LANES), jnp.float32)
        for w in range(nwell):
            entry = jnp.where(well_own == w, inverse[e, w], entry)
        block_out[e] = entry


def maps_kernel(
    areas, nperf, tiles, pivot, lower, upper, well,
    send, cross_out, state_out, order, place_out, rest, states, maps, group,
):
    place_all, place_own = tile_places(areas, nperf, tiles)
    mine = (iota((areas, LANES), 0) == own_area()) & (place_all >= 0)
    flag_lane = jnp.sum(jnp.where(mine, 1.0, 0.0), axis=0, keepdims=True)
    flag_lane = jnp.broadcast_to(flag_lane, (ROWS, LANES))
    row_order(flag_lane, jnp.where(place_own >= 0, 1.0, 0.0), order, place_out, group)
    top = DEPTH - 1
    halves = [slice(0, 8), slice(8, 16)]

    def load(ref, k, h):
        return [ref[c, k, halves[h], :] for c in range(9)]

    state = [None, None]
    for k in range(DEPTH):
        for h in range(2):
            low = load(lower, k, h)
            state[h] = neg(mat(load(pivot, k, h), low if k == 0 else mat(low, state[h])))
            for c in range(9):
                states[h, c, k] = state[h][c]
    down, cross = list(state), list(state)
    well_state, well_cross = [None, None], [None, None]
    for k in reversed(range(DEPTH)):
        for h in range(2):
            both = mat(load(pivot, k, h), load(upper, k, h))
            if k == top:
                state[h] = neg(both)
            else:
                cross[h] = sub([states[h, c, k] for c in range(9)], mat(both, cross[h]))
                state[h] = neg(mat(both, state[h]))
            coef = load(well, k, h)
            more_state, more_cross = mat(coef, state[h]), mat(coef, cross[h])
            well_state[h] = more_state if k == top else add(well_state[h], more_state)
            well_cross[h] = more_cross if k == top else add(well_cross[h], more_cross)
            for c in range(9):
                cross_out[c, k, halves[h], :] = cross[h][c]
                state_out[c, k, halves[h], :] = state[h][c]
    for h in range(2):
        for e in range(9):
            maps[e, halves[h], :] = down[h][e]
            maps[9 + e, halves[h], :] = state[h][e]
            maps[18 + e, halves[h], :] = cross[h][e]
            maps[27 + e, halves[h], :] = well_cross[h][e]
            maps[36 + e, halves[h], :] = well_state[h][e]
    for h in range(2):
        at = slice(8 * h, 8 * h + 8)

        def take(e, index):
            return placed(maps[e, 0:8, :], maps[e, 8:16, :], index[at, :])

        down = [take(e, order) for e in range(9)]
        state = [take(9 + e, order) for e in range(9)]
        cross = [take(18 + e, order) for e in range(9)]
        wells = [take(27 + e, group) for e in range(18)]
        put(send, h, 0, down[:4] + state[:4])
        put(send, h, 1, down[4:8] + state[4:8])
        put(send, h, 2, [down[8], cross[0], cross[2], cross[4], state[8], cross[1], cross[3], cross[5]])
        rest[0, at, :] = cross[6]
        rest[1, at, :] = cross[7]
        j = iota((8, LANES), 0) & 3
        behind = []
        for b in range(7):
            value = jnp.where(j == 0, wells[b], wells[7 + b])
            behind.append(value if b > 3 else jnp.where(j == 2, wells[14 + b], value))
        put(send, h, WELLS, [cross[8]] + behind)


def trial_kernel(
    x_in, right_in, left_in, below_in, above_in, rhs, guess, diag, couple, pivot, lower, upper, well, order, rest, sent,
    send, trial_out, well_out, forward, ends,
):
    region = lax.axis_index("region")
    column = lax.axis_index("column")
    layer = lax.axis_index("layer")
    n_column = lax.axis_size("column")
    n_layer = lax.axis_size("layer")
    lane = iota((8, LANES), 1)
    row = iota((8, LANES), 0)
    top = DEPTH - 1
    well_sums = jnp.zeros((8, LANES), jnp.float32)
    halves = [slice(0, 8), slice(8, 16)]
    edges_right = [jnp.where(column > 0, right_in[at, :], 0.0) for at in halves]
    edges_left = [jnp.where(column < n_column - 1, left_in[at, :], 0.0) for at in halves]

    def load(ref, k, h, count=9):
        return [ref[c, k, halves[h], :] for c in range(count)]

    def residual(k, h):
        at, edge_right, edge_left = halves[h], edges_right[h], edges_left[h]
        mid = load(guess, k, h, 3)
        out = vec(load(diag, k, h), mid)
        for c in range(3):
            g = mid[c]
            place = c * DEPTH + k
            x_row = x_in[place : place + 1, :]
            if h == 0:
                outer = jnp.where(region > 0, x_row, 0.0)
                below = jnp.where(row == 0, outer, pltpu.roll(g, 1, 0))
                above = guess[c, k, 1:9, :]
            else:
                outer = jnp.where(region == 0, x_row, 0.0)
                below = guess[c, k, 7:15, :]
                above = jnp.where(row == 7, outer, pltpu.roll(g, 7, 0))
            first = pltpu.roll(edge_right, LANES - place, 1) if place else edge_right
            before = jnp.where(lane == 0, first, pltpu.roll(g, 1, 1))
            last = pltpu.roll(edge_left, LANES - 1 - place, 1)
            after = jnp.where(lane == LANES - 1, last, pltpu.roll(g, LANES - 1, 1))
            beside = below + above + before + after
            if k > 0:
                beside = beside + guess[c, k - 1, at, :]
            else:
                beside = beside + jnp.where(layer > 0, below_in[c, at, :], 0.0)
            if k < top:
                beside = beside + guess[c, k + 1, at, :]
            else:
                beside = beside + jnp.where(layer < n_layer - 1, above_in[c, at, :], 0.0)
            out[c] = rhs[c, k, at, :] - (out[c] - couple[c, k, at, :] * beside)
        return out

    f = [None, None]
    for k in range(DEPTH):
        for h in range(2):
            res = residual(k, h)
            if k > 0:
                res = sub(res, vec(load(lower, k, h), f[h]))
            f[h] = vec(load(pivot, k, h), res)
            for c in range(3):
                forward[h, c, k] = f[h][c]
    s, well_const = list(f), [None, None]
    for k in reversed(range(DEPTH)):
        for h in range(2):
            if k < top:
                more = vec(load(pivot, k, h), vec(load(upper, k, h), s[h]))
                s[h] = sub([forward[h, c, k] for c in range(3)], more)
            more = vec(load(well, k, h), s[h])
            well_const[h] = more if k == top else add(well_const[h], more)
            for c in range(3):
                trial_out[c, k, halves[h], :] = s[h][c]
    for h in range(2):
        for c in range(3):
            ends[c, halves[h], :] = f[h][c]
            ends[3 + c, halves[h], :] = s[h][c]
            total = lane_sum(well_const[h][c])
            well_sums = well_sums + jnp.where(lane == c * ROWS + 8 * h + row, total, 0.0)
    for h in range(2):
        at = slice(8 * h, 8 * h + 8)
        source = [placed(ends[c, 0:8, :], ends[c, 8:16, :], order[at, :]) for c in range(6)]
        put(send, h, TRIAL, source[:3] + [rest[0, at, :]] + source[3:] + [rest[1, at, :]])
    well_out[...] = jnp.broadcast_to(jnp.sum(well_sums, axis=0, keepdims=True), (8, LANES))


def chain_kernel(peers, got, well_sums, order_in, send, step_ref, base_ref, inflow_ref):
    layer = lax.axis_index("layer")
    is_left = iota((peers, LANES), 1) < HALF

    def rows(m):
        return [got[pl.ds(4 * m + j, peers, PACK), :] for j in range(4)]

    def turn(x):
        return pltpu.roll(x, HALF, 1)

    def chain(base, order):
        for c in range(3):
            base_ref[c] = base[c]
        x = [jnp.zeros((1, LANES), jnp.float32)] * 3
        for d in order:
            at = slice(d, d + 1)
            for c in range(3):
                inflow_ref[c, at, :] = x[c]
            step = [step_ref[e, at, :] for e in range(9)]
            x = [
                (base_ref[i, at, :] + step[3 * i] * x[0]) + (step[3 * i + 1] * x[1] + step[3 * i + 2] * x[2])
                for i in range(3)
            ]
        return [inflow_ref[c] for c in range(3)]

    sets = [swapped(rows(m), (1, 2)) for m in range(4)]
    for e in range(9):
        step_ref[e] = sets[e // 4][e % 4]
    source = sets[TRIAL][:3]
    last = rows(WELLS)
    mixed = []
    for pair in sets[2][1:] + [sets[TRIAL][3], swapped(last, (1, 2))[0]]:
        mixed += [turn(pair), pair]
    down = chain(source, range(peers))
    up_base = add(source, vec(mixed[:9], [turn(x) for x in down]))
    up = chain(up_base, reversed(range(peers)))
    both = [jnp.where(is_left, a, b) for a, b in zip(down, up)]
    block = iota((peers, LANES), 1) // BLOCK
    parts = []
    for j in range(3):
        factor = jnp.zeros((peers, LANES), jnp.float32)
        for b in range(7):
            w = 7 * j + b
            if w < 18:
                shift = BLOCK * (b + 1 - (0 if w < 9 else 4)) % LANES
                value = both[w % 3]
                factor = jnp.where(block == b + 1, pltpu.roll(value, shift, 1) if shift else value, factor)
        parts.append(jnp.sum(last[j] * factor, axis=0, keepdims=True))
    mine = well_sums[0:1, :]
    one = iota((1, LANES), 1)
    leader = order_in[pl.ds(4 * (layer // ACROSS), 1), :]
    for c in range(3):
        total = jnp.zeros((1, LANES), jnp.float32)
        for j in range(3):
            for b in range(7):
                w = 7 * j + b
                if w < 18 and (w % 9) // 3 == c:
                    total = total + jnp.where(one // BLOCK == b + 1, parts[j], 0.0)
        mine = mine + jnp.where(one == c * ROWS + leader, lane_sum(total), 0.0)
        send[pl.ds(c, peers, BACK), :] = both[c]
    send[pl.ds(3, peers, BACK), :] = jnp.broadcast_to(mine, (peers, LANES))


def sums_kernel(peers, got, sums):
    total = jnp.sum(got[pl.ds(3, peers, BACK), :], axis=0, keepdims=True)
    sums[...] = jnp.broadcast_to(total, (8, LANES))


def solved_kernel(
    areas, nperf, nwell, tiles, counts, inverse, got, cross, state, trial, place_in,
    solved, same_out, block_out, inflow,
):
    well_masks(areas, nperf, nwell, tiles, counts, inverse, same_out, block_out)
    for c in range(3):
        parts = [got[pl.ds(e * BACK + c, GROUPS, ACROSS * BACK), :] for e in range(ACROSS)]
        for i, part in enumerate(swapped(parts, (1, 2, 4))):
            inflow[3 * (i // 4) + c, pl.ds(i % 4, GROUPS, 4), :] = part

    def rows_of(c):
        low, high = inflow[c, 0:8, :], inflow[c, 8:16, :]
        return jnp.concatenate(
            [placed(low, high, place_in[0:8, :]), placed(low, high, place_in[8:16, :])], axis=0
        )

    u = [rows_of(c) for c in range(3)]
    w = [rows_of(3 + c) for c in range(3)]
    for k in range(DEPTH):
        part = add(vec([cross[e, k] for e in range(9)], u), vec([state[e, k] for e in range(9)], w))
        for c in range(3):
            solved[c, k] = trial[c, k] + part[c]


def pair_kernel(mine, other, out):
    region = lax.axis_index("region")
    out[0:1, :] = jnp.where(region == 0, mine[0:1, :], other[0:1, :])
    out[1:8, :] = jnp.where(region == 0, other[1:8, :], mine[1:8, :])


def wells_kernel(near, after, before, across, same, block, solved, well, out, held, sems):
    gathered = jnp.zeros((ROWS, LANES), jnp.float32)
    column = lax.axis_index("column")
    n_column = lax.axis_size("column")
    for by, sums in enumerate((near, after, across, before)):
        at = lax.rem(column + by, n_column)
        for r in range(2):
            gathered = gathered + jnp.where(same[r * n_column + at] > 0.0, sums[r : r + 1, :], 0.0)
    wide = iota((ROWS, LANES), 1)
    totals = [
        jnp.sum(
            jnp.where((wide >= c * ROWS) & (wide < (c + 1) * ROWS), gathered, 0.0),
            axis=1,
            keepdims=True,
        )
        for c in range(3)
    ]
    rate = vec([block[e] for e in range(9)], totals)
    copies = [pltpu.make_async_copy(held.at[c], out.at[c], sems.at[c]) for c in range(3)]
    for c in range(3):
        for k in range(DEPTH):
            held[c, k] = solved[c, k] - (
                well[c, k] * rate[0] + well[3 + c, k] * rate[1] + well[6 + c, k] * rate[2]
            )
        copies[c].start()
    for copy in copies:
        copy.wait()


def f32(*shape):
    return jax.ShapeDtypeStruct(shape, jnp.float32)


VMEM = pl.BlockSpec(memory_space=pltpu.VMEM)
SMEM = pl.BlockSpec(memory_space=pltpu.SMEM)
LONG = pl.CostEstimate(flops=20_000_000, bytes_accessed=8_000_000, transcendentals=0)
FIRST = pl.CostEstimate(flops=20_000_000_000, bytes_accessed=80_000_000, transcendentals=0)


def call(kernel, out_shape, in_specs, scratch=(), cost=None, aliases=None, out_space=None):
    return pl.pallas_call(
        kernel,
        out_shape=out_shape,
        in_specs=in_specs,
        out_specs=jax.tree.map(lambda _: out_space or VMEM, out_shape),
        scratch_shapes=scratch,
        cost_estimate=cost,
        input_output_aliases=aliases or {},
        compiler_params=pltpu.CompilerParams(vmem_limit_bytes=32 * 1024 * 1024),
    )


def moved(value, axis, by):
    count = lax.axis_size(axis)
    return lax.ppermute(value, axis, [(i, (i + by) % count) for i in range(count)])


def exchanged(value, axes):
    return lax.all_to_all(value, axes, split_axis=0, concat_axis=0, tiled=True)


def local(rhs, guess, diag, couple, pivot, lower, upper, well, inverse, tiles, counts):
    peers = lax.axis_size("layer")
    areas = lax.axis_size(AREA)
    cells = (DEPTH, ROWS, LANES)
    x_face, right_face, left_face, top_face, bottom_face = call(
        edges_kernel,
        (
            f32(3 * DEPTH, LANES), f32(ROWS, LANES), f32(ROWS, LANES),
            f32(3, ROWS, LANES), f32(3, ROWS, LANES),
        ),
        [VMEM],
        cost=FIRST,
    )(guess)
    below_in = moved(top_face, "layer", 1)
    above_in = moved(bottom_face, "layer", -1)
    right_in = moved(right_face, "column", 1)
    left_in = moved(left_face, "column", -1)
    x_in = moved(x_face, "region", 1)
    nine, three = f32(9, *cells), f32(3, *cells)
    index = jax.ShapeDtypeStruct((ROWS, LANES), jnp.int32)
    send, cross, state, order, place, rest = call(
        lambda *refs: maps_kernel(areas, tiles.shape[0], *refs),
        (
            f32(peers * PACK, LANES), nine, nine, index, index, f32(2, ROWS, LANES),
        ),
        [SMEM] + [VMEM] * 4,
        [
            pltpu.VMEM((2, 9, DEPTH, 8, LANES), jnp.float32),
            pltpu.VMEM((45, ROWS, LANES), jnp.float32),
            pltpu.VMEM((ROWS, LANES), jnp.int32),
        ],
        cost=LONG,
    )(tiles, pivot, lower, upper, well)
    send, trial, well_sums = call(
        trial_kernel,
        (f32(peers * PACK, LANES), three, f32(8, LANES)),
        [VMEM] * 16,
        [pltpu.VMEM((2, 3, DEPTH, 8, LANES), jnp.float32), pltpu.VMEM((6, ROWS, LANES), jnp.float32)],
        aliases={15: 0},
    )(x_in, right_in, left_in, below_in, above_in, rhs, guess, diag, couple, pivot, lower, upper, well, order, rest, send)
    got = exchanged(send.reshape(peers, PACK, 1, LANES), "layer").reshape(peers * PACK, LANES)
    back = call(
        lambda *refs: chain_kernel(peers, *refs),
        f32(peers * BACK, LANES),
        [VMEM] * 3,
        [
            pltpu.VMEM((9, peers, LANES), jnp.float32),
            pltpu.VMEM((3, peers, LANES), jnp.float32),
            pltpu.VMEM((3, peers, LANES), jnp.float32),
        ],
    )(got, well_sums, order)
    got = exchanged(back.reshape(peers, BACK, 1, LANES), "layer").reshape(peers * BACK, LANES)
    sums = call(lambda *refs: sums_kernel(peers, *refs), f32(8, LANES), [VMEM])(got)
    near = call(pair_kernel, f32(8, LANES), [VMEM] * 2)(sums, moved(sums, "region", 1))
    after, before, across = [moved(near, "column", by) for by in (-1, 1, 2)]
    solved, same, block = call(
        lambda *refs: solved_kernel(areas, tiles.shape[0], counts.shape[0], *refs),
        (three, f32(areas, ROWS, LANES), f32(9, ROWS, LANES)),
        [SMEM] * 3 + [VMEM] * 5,
        [pltpu.VMEM((6, ROWS, LANES), jnp.float32)],
        cost=LONG,
    )(tiles, counts, inverse, got, cross, state, trial, place)
    return call(
        wells_kernel,
        three,
        [VMEM] * 8,
        [pltpu.VMEM((3, *cells), jnp.float32), pltpu.SemaphoreType.DMA((3,))],
        out_space=pl.BlockSpec(memory_space=pl.ANY),
    )(near, after, before, across, same, block, solved, well)


def solution(mesh):
    cells = P(None, "layer", "region", "column")
    return jax.shard_map(
        local,
        mesh=mesh,
        in_specs=(cells,) * 8 + (P(),) * 3,
        out_specs=cells,
        check_vma=False,
    )
```

```python
import jax
import jax.numpy as jnp
from jax import lax
from jax.experimental import pallas as pl
from jax.experimental.pallas import tpu as pltpu
from jax.sharding import PartitionSpec as P

AREA = ("region", "column")
DEPTH, ROWS, LANES = 8, 16, 128
HALF = LANES // 2
BLOCK = 16
GROUPS, ACROSS = 4, 8
PACK = 19
BACK = 4

TRIAL, WELLS = 3, 4


def mat(a, b):
    return [
        a[3 * i] * b[m] + a[3 * i + 1] * b[3 + m] + a[3 * i + 2] * b[6 + m]
        for i in range(3)
        for m in range(3)
    ]


def vec(a, x):
    return [a[3 * i] * x[0] + a[3 * i + 1] * x[1] + a[3 * i + 2] * x[2] for i in range(3)]


def neg(a):
    return [-entry for entry in a]


def add(a, b):
    return [x + y for x, y in zip(a, b)]


def sub(a, b):
    return [x - y for x, y in zip(a, b)]


def iota(shape, axis):
    return lax.broadcasted_iota(jnp.int32, shape, axis)


def edges_kernel(guess, x_out, right_out, left_out, top_out, bottom_out):
    region = lax.axis_index("region")
    lane = iota((ROWS, LANES), 1)
    right = jnp.zeros((ROWS, LANES), jnp.float32)
    left = jnp.zeros((ROWS, LANES), jnp.float32)
    for c in range(3):
        for k in range(DEPTH):
            place = c * DEPTH + k
            block = guess[c, k]
            right = jnp.where(lane == place, pltpu.roll(block, (place + 1) % LANES, 1), right)
            left = jnp.where(lane == place, pltpu.roll(block, place, 1) if place else block, left)
            x_out[place : place + 1, :] = jnp.where(
                region == 0, guess[c, k, ROWS - 1 :, :], guess[c, k, :1, :]
            )
        top_out[c] = guess[c, DEPTH - 1]
        bottom_out[c] = guess[c, 0]
    right_out[...] = right
    left_out[...] = left


def swapped(parts, steps):
    parts = list(parts)
    for step in steps:
        block = iota(parts[0].shape, 1) // BLOCK
        low = (block & step) == 0
        for i in range(len(parts)):
            if i & step == 0:
                a, b = parts[i], parts[i + step]
                parts[i] = jnp.where(low, a, pltpu.roll(b, BLOCK * step, 1))
                parts[i + step] = jnp.where(low, pltpu.roll(a, LANES - BLOCK * step, 1), b)
    return parts


def placed(low, high, index):
    inner = index & 7
    return jnp.where(
        index < 8,
        jnp.take_along_axis(low, inner, axis=0, mode="promise_in_bounds"),
        jnp.take_along_axis(high, inner, axis=0, mode="promise_in_bounds"),
    )


def put(send, h, m, parts, count=4):
    for e, part in enumerate(swapped(parts, (1, 2, 4))):
        for half in range(2):
            at = (ACROSS * (2 * h + half) + e) * PACK + 4 * m
            send[at : at + count, :] = part[4 * half : 4 * half + count, :]


def lane_sum(x):
    return jnp.sum(x, axis=1, keepdims=True)


def row_order(flag_lane, flag_row, order_out, place_out, group_out):
    row = iota((ROWS, LANES), 0)
    lane = iota((ROWS, LANES), 1)
    inner = lane % ROWS

    def place_of(flag, rank, number):
        free = number - rank
        return jnp.where(flag > 0.0, 4 * rank, free + 1 + ((free * 11) >> 5))

    rank_row = lane_sum(jnp.where((lane < ROWS) & (lane < row), flag_lane, 0.0))
    rank_lane = jnp.sum(jnp.where(row < inner, flag_row, 0.0), axis=0, keepdims=True)
    rank_row = jnp.broadcast_to(rank_row, (ROWS, LANES)).astype(jnp.int32)
    rank_lane = jnp.broadcast_to(rank_lane, (ROWS, LANES)).astype(jnp.int32)
    place_out[...] = place_of(flag_row, rank_row, row)
    at_lane = place_of(flag_lane, rank_lane, inner)
    number = jnp.where(lane < ROWS, lane, 0).astype(jnp.float32)
    for out, wanted in ((order_out, row), (group_out, row & 12)):
        found = lane_sum(jnp.where(at_lane == wanted, number, 0.0))
        out[...] = jnp.broadcast_to(found, (ROWS, LANES)).astype(jnp.int32)


def own_area():
    return lax.axis_index("region") * lax.axis_size("column") + lax.axis_index("column")


def tile_places(areas, nperf, tiles):
    tile_all = iota((areas, LANES), 0) * ROWS + iota((areas, LANES), 1) % ROWS
    tile_own = own_area() * ROWS + iota((ROWS, LANES), 0)
    place_all = jnp.full((areas, LANES), -1, jnp.int32)
    place_own = jnp.full((ROWS, LANES), -1, jnp.int32)
    for p in range(nperf):
        place_all = jnp.where(tile_all == tiles[p], p, place_all)
        place_own = jnp.where(tile_own == tiles[p], p, place_own)
    return place_all, place_own


def well_masks(areas, nperf, nwell, tiles, counts, inverse, same_out, block_out):
    place_all, place_own = tile_places(areas, nperf, tiles)
    well_all = jnp.where(place_all < 0, -1, 0)
    well_own = jnp.where(place_own < 0, -2, 0)
    end = 0
    for w in range(nwell):
        end = end + counts[w]
        well_all = well_all + (place_all >= end).astype(jnp.int32)
        well_own = well_own + (place_own >= end).astype(jnp.int32)
    for a in range(areas):
        same_out[a] = (well_own == well_all[a : a + 1, :]).astype(jnp.float32)
    for e in range(9):
        entry = jnp.zeros((ROWS, LANES), jnp.float32)
        for w in range(nwell):
            entry = jnp.where(well_own == w, inverse[e, w], entry)
        block_out[e] = entry


def maps_kernel(
    areas, nperf, tiles, pivot, lower, upper, well,
    send, cross_out, state_out, order, place_out, rest, states, maps, group,
):
    place_all, place_own = tile_places(areas, nperf, tiles)
    mine = (iota((areas, LANES), 0) == own_area()) & (place_all >= 0)
    flag_lane = jnp.sum(jnp.where(mine, 1.0, 0.0), axis=0, keepdims=True)
    flag_lane = jnp.broadcast_to(flag_lane, (ROWS, LANES))
    row_order(flag_lane, jnp.where(place_own >= 0, 1.0, 0.0), order, place_out, group)
    top = DEPTH - 1
    halves = [slice(0, 8), slice(8, 16)]

    def load(ref, k, h):
        return [ref[c, k, halves[h], :] for c in range(9)]

    state = [None, None]
    for k in range(DEPTH):
        for h in range(2):
            low = load(lower, k, h)
            state[h] = neg(mat(load(pivot, k, h), low if k == 0 else mat(low, state[h])))
            for c in range(9):
                states[h, c, k] = state[h][c]
    down, cross = list(state), list(state)
    well_state, well_cross = [None, None], [None, None]
    for k in reversed(range(DEPTH)):
        for h in range(2):
            both = mat(load(pivot, k, h), load(upper, k, h))
            if k == top:
                state[h] = neg(both)
            else:
                cross[h] = sub([states[h, c, k] for c in range(9)], mat(both, cross[h]))
                state[h] = neg(mat(both, state[h]))
            coef = load(well, k, h)
            more_state, more_cross = mat(coef, state[h]), mat(coef, cross[h])
            well_state[h] = more_state if k == top else add(well_state[h], more_state)
            well_cross[h] = more_cross if k == top else add(well_cross[h], more_cross)
            for c in range(9):
                cross_out[c, k, halves[h], :] = cross[h][c]
                state_out[c, k, halves[h], :] = state[h][c]
    for h in range(2):
        for e in range(9):
            maps[e, halves[h], :] = down[h][e]
            maps[9 + e, halves[h], :] = state[h][e]
            maps[18 + e, halves[h], :] = cross[h][e]
            maps[27 + e, halves[h], :] = well_cross[h][e]
            maps[36 + e, halves[h], :] = well_state[h][e]
    for h in range(2):
        at = slice(8 * h, 8 * h + 8)

        def take(e, index):
            return placed(maps[e, 0:8, :], maps[e, 8:16, :], index[at, :])

        down = [take(e, order) for e in range(9)]
        state = [take(9 + e, order) for e in range(9)]
        cross = [take(18 + e, order) for e in range(9)]
        wells = [take(27 + e, group) for e in range(18)]
        put(send, h, 0, down[:4] + state[:4])
        put(send, h, 1, down[4:8] + state[4:8])
        put(send, h, 2, [down[8], cross[0], cross[2], cross[4], state[8], cross[1], cross[3], cross[5]])
        rest[0, at, :] = cross[6]
        rest[1, at, :] = cross[7]
        j = iota((8, LANES), 0) & 3
        behind = []
        for b in range(7):
            value = jnp.where(j == 0, wells[b], wells[7 + b])
            third = wells[14 + b] if b < 4 else pltpu.roll(cross[8], 7, 0)
            behind.append(jnp.where(j == 2, third, value) if b < 5 else value)
        put(send, h, WELLS, [cross[8]] + behind, 3)


def trial_kernel(
    x_in, right_in, left_in, below_in, above_in, rhs, guess, diag, couple, pivot, lower, upper, well, order, rest, sent,
    send, trial_out, well_out, forward, ends,
):
    region = lax.axis_index("region")
    column = lax.axis_index("column")
    layer = lax.axis_index("layer")
    n_column = lax.axis_size("column")
    n_layer = lax.axis_size("layer")
    lane = iota((8, LANES), 1)
    row = iota((8, LANES), 0)
    top = DEPTH - 1
    well_sums = jnp.zeros((8, LANES), jnp.float32)
    halves = [slice(0, 8), slice(8, 16)]
    edges_right = [jnp.where(column > 0, right_in[at, :], 0.0) for at in halves]
    edges_left = [jnp.where(column < n_column - 1, left_in[at, :], 0.0) for at in halves]

    def load(ref, k, h, count=9):
        return [ref[c, k, halves[h], :] for c in range(count)]

    def residual(k, h):
        at, edge_right, edge_left = halves[h], edges_right[h], edges_left[h]
        mid = load(guess, k, h, 3)
        out = vec(load(diag, k, h), mid)
        for c in range(3):
            g = mid[c]
            place = c * DEPTH + k
            x_row = x_in[place : place + 1, :]
            if h == 0:
                outer = jnp.where(region > 0, x_row, 0.0)
                below = jnp.where(row == 0, outer, pltpu.roll(g, 1, 0))
                above = guess[c, k, 1:9, :]
            else:
                outer = jnp.where(region == 0, x_row, 0.0)
                below = guess[c, k, 7:15, :]
                above = jnp.where(row == 7, outer, pltpu.roll(g, 7, 0))
            first = pltpu.roll(edge_right, LANES - place, 1) if place else edge_right
            before = jnp.where(lane == 0, first, pltpu.roll(g, 1, 1))
            last = pltpu.roll(edge_left, LANES - 1 - place, 1)
            after = jnp.where(lane == LANES - 1, last, pltpu.roll(g, LANES - 1, 1))
            beside = below + above + before + after
            if k > 0:
                beside = beside + guess[c, k - 1, at, :]
            else:
                beside = beside + jnp.where(layer > 0, below_in[c, at, :], 0.0)
            if k < top:
                beside = beside + guess[c, k + 1, at, :]
            else:
                beside = beside + jnp.where(layer < n_layer - 1, above_in[c, at, :], 0.0)
            out[c] = rhs[c, k, at, :] - (out[c] - couple[c, k, at, :] * beside)
        return out

    f = [None, None]
    for k in range(DEPTH):
        for h in range(2):
            res = residual(k, h)
            if k > 0:
                res = sub(res, vec(load(lower, k, h), f[h]))
            f[h] = vec(load(pivot, k, h), res)
            for c in range(3):
                forward[h, c, k] = f[h][c]
    s, well_const = list(f), [None, None]
    for k in reversed(range(DEPTH)):
        for h in range(2):
            if k < top:
                more = vec(load(pivot, k, h), vec(load(upper, k, h), s[h]))
                s[h] = sub([forward[h, c, k] for c in range(3)], more)
            more = vec(load(well, k, h), s[h])
            well_const[h] = more if k == top else add(well_const[h], more)
            for c in range(3):
                trial_out[c, k, halves[h], :] = s[h][c]
    for h in range(2):
        for c in range(3):
            ends[c, halves[h], :] = f[h][c]
            ends[3 + c, halves[h], :] = s[h][c]
            total = lane_sum(well_const[h][c])
            well_sums = well_sums + jnp.where(lane == c * ROWS + 8 * h + row, total, 0.0)
    for h in range(2):
        at = slice(8 * h, 8 * h + 8)
        source = [placed(ends[c, 0:8, :], ends[c, 8:16, :], order[at, :]) for c in range(6)]
        put(send, h, TRIAL, source[:3] + [rest[0, at, :]] + source[3:] + [rest[1, at, :]])
    well_out[...] = jnp.broadcast_to(jnp.sum(well_sums, axis=0, keepdims=True), (8, LANES))


def chain_kernel(peers, got, well_sums, order_in, send, step_ref, base_ref, inflow_ref):
    layer = lax.axis_index("layer")
    is_left = iota((peers, LANES), 1) < HALF

    def rows(m, count=4):
        return [got[pl.ds(4 * m + j, peers, PACK), :] for j in range(count)]

    def turn(x):
        return pltpu.roll(x, HALF, 1)

    def chain(base, order):
        for c in range(3):
            base_ref[c] = base[c]
        x = [jnp.zeros((1, LANES), jnp.float32)] * 3
        for d in order:
            at = slice(d, d + 1)
            for c in range(3):
                inflow_ref[c, at, :] = x[c]
            step = [step_ref[e, at, :] for e in range(9)]
            x = [
                (base_ref[i, at, :] + step[3 * i] * x[0]) + (step[3 * i + 1] * x[1] + step[3 * i + 2] * x[2])
                for i in range(3)
            ]
        return [inflow_ref[c] for c in range(3)]

    sets = [swapped(rows(m), (1, 2)) for m in range(4)]
    for e in range(9):
        step_ref[e] = sets[e // 4][e % 4]
    source = sets[TRIAL][:3]
    last = rows(WELLS, 3)
    fourth = pltpu.roll(last[2], LANES - 5 * BLOCK, 1)
    mixed = []
    for pair in sets[2][1:] + [sets[TRIAL][3], swapped(last + [fourth], (1, 2))[0]]:
        mixed += [turn(pair), pair]
    down = chain(source, range(peers))
    up_base = add(source, vec(mixed[:9], [turn(x) for x in down]))
    up = chain(up_base, reversed(range(peers)))
    both = [jnp.where(is_left, a, b) for a, b in zip(down, up)]
    block = iota((peers, LANES), 1) // BLOCK
    parts = []
    for j in range(3):
        factor = jnp.zeros((peers, LANES), jnp.float32)
        for b in range(7):
            w = 7 * j + b
            if w < 18:
                shift = BLOCK * (b + 1 - (0 if w < 9 else 4)) % LANES
                value = both[w % 3]
                factor = jnp.where(block == b + 1, pltpu.roll(value, shift, 1) if shift else value, factor)
        parts.append(jnp.sum(last[j] * factor, axis=0, keepdims=True))
    mine = well_sums[0:1, :]
    one = iota((1, LANES), 1)
    leader = order_in[pl.ds(4 * (layer // ACROSS), 1), :]
    for c in range(3):
        total = jnp.zeros((1, LANES), jnp.float32)
        for j in range(3):
            for b in range(7):
                w = 7 * j + b
                if w < 18 and (w % 9) // 3 == c:
                    total = total + jnp.where(one // BLOCK == b + 1, parts[j], 0.0)
        mine = mine + jnp.where(one == c * ROWS + leader, lane_sum(total), 0.0)
        send[pl.ds(c, peers, BACK), :] = both[c]
    send[pl.ds(3, peers, BACK), :] = jnp.broadcast_to(mine, (peers, LANES))


def sums_kernel(peers, got, sums):
    total = jnp.sum(got[pl.ds(3, peers, BACK), :], axis=0, keepdims=True)
    sums[...] = jnp.broadcast_to(total, (8, LANES))


def solved_kernel(
    areas, nperf, nwell, tiles, counts, inverse, got, cross, state, trial, place_in,
    solved, same_out, block_out, inflow,
):
    well_masks(areas, nperf, nwell, tiles, counts, inverse, same_out, block_out)
    for c in range(3):
        parts = [got[pl.ds(e * BACK + c, GROUPS, ACROSS * BACK), :] for e in range(ACROSS)]
        for i, part in enumerate(swapped(parts, (1, 2, 4))):
            inflow[3 * (i // 4) + c, pl.ds(i % 4, GROUPS, 4), :] = part

    def rows_of(c):
        low, high = inflow[c, 0:8, :], inflow[c, 8:16, :]
        return jnp.concatenate(
            [placed(low, high, place_in[0:8, :]), placed(low, high, place_in[8:16, :])], axis=0
        )

    u = [rows_of(c) for c in range(3)]
    w = [rows_of(3 + c) for c in range(3)]
    for k in range(DEPTH):
        part = add(vec([cross[e, k] for e in range(9)], u), vec([state[e, k] for e in range(9)], w))
        for c in range(3):
            solved[c, k] = trial[c, k] + part[c]


def pair_kernel(mine, other, out):
    region = lax.axis_index("region")
    out[0:1, :] = jnp.where(region == 0, mine[0:1, :], other[0:1, :])
    out[1:8, :] = jnp.where(region == 0, other[1:8, :], mine[1:8, :])


def wells_kernel(near, after, before, across, same, block, solved, well, out, held, sems):
    gathered = jnp.zeros((ROWS, LANES), jnp.float32)
    column = lax.axis_index("column")
    n_column = lax.axis_size("column")
    for by, sums in enumerate((near, after, across, before)):
        at = lax.rem(column + by, n_column)
        for r in range(2):
            gathered = gathered + jnp.where(same[r * n_column + at] > 0.0, sums[r : r + 1, :], 0.0)
    wide = iota((ROWS, LANES), 1)
    totals = [
        jnp.sum(
            jnp.where((wide >= c * ROWS) & (wide < (c + 1) * ROWS), gathered, 0.0),
            axis=1,
            keepdims=True,
        )
        for c in range(3)
    ]
    rate = vec([block[e] for e in range(9)], totals)
    copies = [pltpu.make_async_copy(held.at[c], out.at[c], sems.at[c]) for c in range(3)]
    for c in range(3):
        for k in range(DEPTH):
            held[c, k] = solved[c, k] - (
                well[c, k] * rate[0] + well[3 + c, k] * rate[1] + well[6 + c, k] * rate[2]
            )
        copies[c].start()
    for copy in copies:
        copy.wait()


def f32(*shape):
    return jax.ShapeDtypeStruct(shape, jnp.float32)


VMEM = pl.BlockSpec(memory_space=pltpu.VMEM)
SMEM = pl.BlockSpec(memory_space=pltpu.SMEM)
LONG = pl.CostEstimate(flops=20_000_000, bytes_accessed=8_000_000, transcendentals=0)
FIRST = pl.CostEstimate(flops=20_000_000_000, bytes_accessed=80_000_000, transcendentals=0)


def call(kernel, out_shape, in_specs, scratch=(), cost=None, aliases=None, out_space=None):
    return pl.pallas_call(
        kernel,
        out_shape=out_shape,
        in_specs=in_specs,
        out_specs=jax.tree.map(lambda _: out_space or VMEM, out_shape),
        scratch_shapes=scratch,
        cost_estimate=cost,
        input_output_aliases=aliases or {},
        compiler_params=pltpu.CompilerParams(vmem_limit_bytes=32 * 1024 * 1024),
    )


def moved(value, axis, by):
    count = lax.axis_size(axis)
    return lax.ppermute(value, axis, [(i, (i + by) % count) for i in range(count)])


def exchanged(value, axes):
    return lax.all_to_all(value, axes, split_axis=0, concat_axis=0, tiled=True)


def local(rhs, guess, diag, couple, pivot, lower, upper, well, inverse, tiles, counts):
    peers = lax.axis_size("layer")
    areas = lax.axis_size(AREA)
    cells = (DEPTH, ROWS, LANES)
    x_face, right_face, left_face, top_face, bottom_face = call(
        edges_kernel,
        (
            f32(3 * DEPTH, LANES), f32(ROWS, LANES), f32(ROWS, LANES),
            f32(3, ROWS, LANES), f32(3, ROWS, LANES),
        ),
        [VMEM],
        cost=FIRST,
    )(guess)
    below_in = moved(top_face, "layer", 1)
    above_in = moved(bottom_face, "layer", -1)
    right_in = moved(right_face, "column", 1)
    left_in = moved(left_face, "column", -1)
    x_in = moved(x_face, "region", 1)
    nine, three = f32(9, *cells), f32(3, *cells)
    index = jax.ShapeDtypeStruct((ROWS, LANES), jnp.int32)
    send, cross, state, order, place, rest = call(
        lambda *refs: maps_kernel(areas, tiles.shape[0], *refs),
        (
            f32(peers * PACK, LANES), nine, nine, index, index, f32(2, ROWS, LANES),
        ),
        [SMEM] + [VMEM] * 4,
        [
            pltpu.VMEM((2, 9, DEPTH, 8, LANES), jnp.float32),
            pltpu.VMEM((45, ROWS, LANES), jnp.float32),
            pltpu.VMEM((ROWS, LANES), jnp.int32),
        ],
        cost=LONG,
    )(tiles, pivot, lower, upper, well)
    send, trial, well_sums = call(
        trial_kernel,
        (f32(peers * PACK, LANES), three, f32(8, LANES)),
        [VMEM] * 16,
        [pltpu.VMEM((2, 3, DEPTH, 8, LANES), jnp.float32), pltpu.VMEM((6, ROWS, LANES), jnp.float32)],
        aliases={15: 0},
    )(x_in, right_in, left_in, below_in, above_in, rhs, guess, diag, couple, pivot, lower, upper, well, order, rest, send)
    got = exchanged(send.reshape(peers, PACK, 1, LANES), "layer").reshape(peers * PACK, LANES)
    back = call(
        lambda *refs: chain_kernel(peers, *refs),
        f32(peers * BACK, LANES),
        [VMEM] * 3,
        [
            pltpu.VMEM((9, peers, LANES), jnp.float32),
            pltpu.VMEM((3, peers, LANES), jnp.float32),
            pltpu.VMEM((3, peers, LANES), jnp.float32),
        ],
    )(got, well_sums, order)
    got = exchanged(back.reshape(peers, BACK, 1, LANES), "layer").reshape(peers * BACK, LANES)
    sums = call(lambda *refs: sums_kernel(peers, *refs), f32(8, LANES), [VMEM])(got)
    near = call(pair_kernel, f32(8, LANES), [VMEM] * 2)(sums, moved(sums, "region", 1))
    after, before, across = [moved(near, "column", by) for by in (-1, 1, 2)]
    solved, same, block = call(
        lambda *refs: solved_kernel(areas, tiles.shape[0], counts.shape[0], *refs),
        (three, f32(areas, ROWS, LANES), f32(9, ROWS, LANES)),
        [SMEM] * 3 + [VMEM] * 5,
        [pltpu.VMEM((6, ROWS, LANES), jnp.float32)],
        cost=LONG,
    )(tiles, counts, inverse, got, cross, state, trial, place)
    return call(
        wells_kernel,
        three,
        [VMEM] * 8,
        [pltpu.VMEM((3, *cells), jnp.float32), pltpu.SemaphoreType.DMA((3,))],
        out_space=pl.BlockSpec(memory_space=pl.ANY),
    )(near, after, before, across, same, block, solved, well)


def solution(mesh):
    cells = P(None, "layer", "region", "column")
    return jax.shard_map(
        local,
        mesh=mesh,
        in_specs=(cells,) * 8 + (P(),) * 3,
        out_specs=cells,
        check_vma=False,
    )
```

```python
import jax
import jax.numpy as jnp
from jax import lax
from jax.experimental import pallas as pl
from jax.experimental.pallas import tpu as pltpu
from jax.sharding import PartitionSpec as P

AREA = ("region", "column")
DEPTH, ROWS, LANES = 8, 16, 128
HALF = LANES // 2
BLOCK = 16
GROUPS, ACROSS = 4, 8
PACK = 19
BACK = 4

TRIAL, WELLS = 3, 4


def mat(a, b):
    return [
        a[3 * i] * b[m] + a[3 * i + 1] * b[3 + m] + a[3 * i + 2] * b[6 + m]
        for i in range(3)
        for m in range(3)
    ]


def vec(a, x):
    return [a[3 * i] * x[0] + a[3 * i + 1] * x[1] + a[3 * i + 2] * x[2] for i in range(3)]


def neg(a):
    return [-entry for entry in a]


def add(a, b):
    return [x + y for x, y in zip(a, b)]


def sub(a, b):
    return [x - y for x, y in zip(a, b)]


def iota(shape, axis):
    return lax.broadcasted_iota(jnp.int32, shape, axis)


def edges_kernel(guess, x_out, right_out, left_out, top_out, bottom_out):
    region = lax.axis_index("region")
    lane = iota((ROWS, LANES), 1)
    right = jnp.zeros((ROWS, LANES), jnp.float32)
    left = jnp.zeros((ROWS, LANES), jnp.float32)
    for c in range(3):
        for k in range(DEPTH):
            place = c * DEPTH + k
            block = guess[c, k]
            right = jnp.where(lane == place, pltpu.roll(block, (place + 1) % LANES, 1), right)
            left = jnp.where(lane == place, pltpu.roll(block, place, 1) if place else block, left)
            x_out[place : place + 1, :] = jnp.where(
                region == 0, guess[c, k, ROWS - 1 :, :], guess[c, k, :1, :]
            )
        top_out[c] = guess[c, DEPTH - 1]
        bottom_out[c] = guess[c, 0]
    right_out[...] = right
    left_out[...] = left


def swapped(parts, steps):
    parts = list(parts)
    for step in steps:
        block = iota(parts[0].shape, 1) // BLOCK
        low = (block & step) == 0
        for i in range(len(parts)):
            if i & step == 0:
                a, b = parts[i], parts[i + step]
                parts[i] = jnp.where(low, a, pltpu.roll(b, BLOCK * step, 1))
                parts[i + step] = jnp.where(low, pltpu.roll(a, LANES - BLOCK * step, 1), b)
    return parts


def placed(low, high, index):
    inner = index & 7
    return jnp.where(
        index < 8,
        jnp.take_along_axis(low, inner, axis=0, mode="promise_in_bounds"),
        jnp.take_along_axis(high, inner, axis=0, mode="promise_in_bounds"),
    )


def put(send, h, m, parts, count=4):
    for e, part in enumerate(swapped(parts, (1, 2, 4))):
        for half in range(2):
            at = (ACROSS * (2 * h + half) + e) * PACK + 4 * m
            send[at : at + count, :] = part[4 * half : 4 * half + count, :]


def lane_sum(x):
    return jnp.sum(x, axis=1, keepdims=True)


def row_order(flag_lane, flag_row, order_out, place_out, group_out):
    row = iota((ROWS, LANES), 0)
    lane = iota((ROWS, LANES), 1)
    inner = lane % ROWS

    def place_of(flag, rank, number):
        free = number - rank
        return jnp.where(flag > 0.0, 4 * rank, free + 1 + ((free * 11) >> 5))

    rank_row = lane_sum(jnp.where((lane < ROWS) & (lane < row), flag_lane, 0.0))
    rank_lane = jnp.sum(jnp.where(row < inner, flag_row, 0.0), axis=0, keepdims=True)
    rank_row = jnp.broadcast_to(rank_row, (ROWS, LANES)).astype(jnp.int32)
    rank_lane = jnp.broadcast_to(rank_lane, (ROWS, LANES)).astype(jnp.int32)
    place_out[...] = place_of(flag_row, rank_row, row)
    at_lane = place_of(flag_lane, rank_lane, inner)
    number = jnp.where(lane < ROWS, lane, 0).astype(jnp.float32)
    for out, wanted in ((order_out, row), (group_out, row & 12)):
        found = lane_sum(jnp.where(at_lane == wanted, number, 0.0))
        out[...] = jnp.broadcast_to(found, (ROWS, LANES)).astype(jnp.int32)


def own_area():
    return lax.axis_index("region") * lax.axis_size("column") + lax.axis_index("column")


def tile_places(areas, nperf, tiles):
    tile_all = iota((areas, LANES), 0) * ROWS + iota((areas, LANES), 1) % ROWS
    tile_own = own_area() * ROWS + iota((ROWS, LANES), 0)
    place_all = jnp.full((areas, LANES), -1, jnp.int32)
    place_own = jnp.full((ROWS, LANES), -1, jnp.int32)
    for p in range(nperf):
        place_all = jnp.where(tile_all == tiles[p], p, place_all)
        place_own = jnp.where(tile_own == tiles[p], p, place_own)
    return place_all, place_own


def well_masks(areas, nperf, nwell, tiles, counts, inverse, same_out, block_out):
    place_all, place_own = tile_places(areas, nperf, tiles)
    well_all = jnp.where(place_all < 0, -1, 0)
    well_own = jnp.where(place_own < 0, -2, 0)
    end = 0
    for w in range(nwell):
        end = end + counts[w]
        well_all = well_all + (place_all >= end).astype(jnp.int32)
        well_own = well_own + (place_own >= end).astype(jnp.int32)
    for a in range(areas):
        same_out[a] = (well_own == well_all[a : a + 1, :]).astype(jnp.float32)
    for e in range(9):
        entry = jnp.zeros((ROWS, LANES), jnp.float32)
        for w in range(nwell):
            entry = jnp.where(well_own == w, inverse[e, w], entry)
        block_out[e] = entry


def maps_kernel(
    areas, nperf, tiles, pivot, lower, upper, well, rhs, guess, diag, couple,
    send, cross_out, state_out, order, place_out, rest, inner, states, maps, group,
):
    place_all, place_own = tile_places(areas, nperf, tiles)
    mine = (iota((areas, LANES), 0) == own_area()) & (place_all >= 0)
    flag_lane = jnp.sum(jnp.where(mine, 1.0, 0.0), axis=0, keepdims=True)
    flag_lane = jnp.broadcast_to(flag_lane, (ROWS, LANES))
    row_order(flag_lane, jnp.where(place_own >= 0, 1.0, 0.0), order, place_out, group)
    top = DEPTH - 1
    halves = [slice(0, 8), slice(8, 16)]

    def load(ref, k, h):
        return [ref[c, k, halves[h], :] for c in range(9)]

    row = iota((8, LANES), 0)
    lane = iota((8, LANES), 1)
    for k in range(DEPTH):
        for h in range(2):
            at = halves[h]
            mid = [guess[c, k, at, :] for c in range(3)]
            out = vec(load(diag, k, h), mid)
            for c in range(3):
                g = mid[c]
                if h == 0:
                    below = jnp.where(row == 0, 0.0, pltpu.roll(g, 1, 0))
                    above = guess[c, k, 1:9, :]
                else:
                    below = guess[c, k, 7:15, :]
                    above = jnp.where(row == 7, 0.0, pltpu.roll(g, 7, 0))
                before = jnp.where(lane == 0, 0.0, pltpu.roll(g, 1, 1))
                after = jnp.where(lane == LANES - 1, 0.0, pltpu.roll(g, LANES - 1, 1))
                beside = below + above + before + after
                if k > 0:
                    beside = beside + guess[c, k - 1, at, :]
                if k < top:
                    beside = beside + guess[c, k + 1, at, :]
                inner[c, k, at, :] = rhs[c, k, at, :] - (out[c] - couple[c, k, at, :] * beside)

    state = [None, None]
    for k in range(DEPTH):
        for h in range(2):
            low = load(lower, k, h)
            state[h] = neg(mat(load(pivot, k, h), low if k == 0 else mat(low, state[h])))
            for c in range(9):
                states[h, c, k] = state[h][c]
    down, cross = list(state), list(state)
    well_state, well_cross = [None, None], [None, None]
    for k in reversed(range(DEPTH)):
        for h in range(2):
            both = mat(load(pivot, k, h), load(upper, k, h))
            if k == top:
                state[h] = neg(both)
            else:
                cross[h] = sub([states[h, c, k] for c in range(9)], mat(both, cross[h]))
                state[h] = neg(mat(both, state[h]))
            coef = load(well, k, h)
            more_state, more_cross = mat(coef, state[h]), mat(coef, cross[h])
            well_state[h] = more_state if k == top else add(well_state[h], more_state)
            well_cross[h] = more_cross if k == top else add(well_cross[h], more_cross)
            for c in range(9):
                cross_out[c, k, halves[h], :] = cross[h][c]
                state_out[c, k, halves[h], :] = state[h][c]
    for h in range(2):
        for e in range(9):
            maps[e, halves[h], :] = down[h][e]
            maps[9 + e, halves[h], :] = state[h][e]
            maps[18 + e, halves[h], :] = cross[h][e]
            maps[27 + e, halves[h], :] = well_cross[h][e]
            maps[36 + e, halves[h], :] = well_state[h][e]
    for h in range(2):
        at = slice(8 * h, 8 * h + 8)

        def take(e, index):
            return placed(maps[e, 0:8, :], maps[e, 8:16, :], index[at, :])

        down = [take(e, order) for e in range(9)]
        state = [take(9 + e, order) for e in range(9)]
        cross = [take(18 + e, order) for e in range(9)]
        wells = [take(27 + e, group) for e in range(18)]
        put(send, h, 0, down[:4] + state[:4])
        put(send, h, 1, down[4:8] + state[4:8])
        put(send, h, 2, [down[8], cross[0], cross[2], cross[4], state[8], cross[1], cross[3], cross[5]])
        rest[0, at, :] = cross[6]
        rest[1, at, :] = cross[7]
        j = iota((8, LANES), 0) & 3
        behind = []
        for b in range(7):
            value = jnp.where(j == 0, wells[b], wells[7 + b])
            third = wells[14 + b] if b < 4 else pltpu.roll(cross[8], 7, 0)
            behind.append(jnp.where(j == 2, third, value) if b < 5 else value)
        put(send, h, WELLS, [cross[8]] + behind, 3)


def trial_kernel(
    x_in, right_in, left_in, below_in, above_in, inner, couple, pivot, lower, upper, well, order, rest, sent,
    send, trial_out, well_out, forward, ends,
):
    region = lax.axis_index("region")
    column = lax.axis_index("column")
    layer = lax.axis_index("layer")
    n_column = lax.axis_size("column")
    n_layer = lax.axis_size("layer")
    lane = iota((8, LANES), 1)
    row = iota((8, LANES), 0)
    top = DEPTH - 1
    well_sums = jnp.zeros((8, LANES), jnp.float32)
    halves = [slice(0, 8), slice(8, 16)]
    edges_right = [jnp.where(column > 0, right_in[at, :], 0.0) for at in halves]
    edges_left = [jnp.where(column < n_column - 1, left_in[at, :], 0.0) for at in halves]

    def load(ref, k, h, count=9):
        return [ref[c, k, halves[h], :] for c in range(count)]

    def residual(k, h):
        at, edge_right, edge_left = halves[h], edges_right[h], edges_left[h]
        out = []
        for c in range(3):
            place = c * DEPTH + k
            x_row = x_in[place : place + 1, :]
            outer = jnp.where(region > 0 if h == 0 else region == 0, x_row, 0.0)
            beside = jnp.where(row == (0 if h == 0 else 7), outer, 0.0)
            first = pltpu.roll(edge_right, LANES - place, 1) if place else edge_right
            last = pltpu.roll(edge_left, LANES - 1 - place, 1)
            ends_y = jnp.where(lane == 0, first, jnp.where(lane == LANES - 1, last, 0.0))
            beside = beside + ends_y
            if k == 0:
                beside = beside + jnp.where(layer > 0, below_in[c, at, :], 0.0)
            if k == top:
                beside = beside + jnp.where(layer < n_layer - 1, above_in[c, at, :], 0.0)
            out.append(inner[c, k, at, :] + couple[c, k, at, :] * beside)
        return out

    f = [None, None]
    for k in range(DEPTH):
        for h in range(2):
            res = residual(k, h)
            if k > 0:
                res = sub(res, vec(load(lower, k, h), f[h]))
            f[h] = vec(load(pivot, k, h), res)
            for c in range(3):
                forward[h, c, k] = f[h][c]
    s, well_const = list(f), [None, None]
    for k in reversed(range(DEPTH)):
        for h in range(2):
            if k < top:
                more = vec(load(pivot, k, h), vec(load(upper, k, h), s[h]))
                s[h] = sub([forward[h, c, k] for c in range(3)], more)
            more = vec(load(well, k, h), s[h])
            well_const[h] = more if k == top else add(well_const[h], more)
            for c in range(3):
                trial_out[c, k, halves[h], :] = s[h][c]
    for h in range(2):
        for c in range(3):
            ends[c, halves[h], :] = f[h][c]
            ends[3 + c, halves[h], :] = s[h][c]
            total = lane_sum(well_const[h][c])
            well_sums = well_sums + jnp.where(lane == c * ROWS + 8 * h + row, total, 0.0)
    for h in range(2):
        at = slice(8 * h, 8 * h + 8)
        source = [placed(ends[c, 0:8, :], ends[c, 8:16, :], order[at, :]) for c in range(6)]
        put(send, h, TRIAL, source[:3] + [rest[0, at, :]] + source[3:] + [rest[1, at, :]])
    well_out[...] = jnp.broadcast_to(jnp.sum(well_sums, axis=0, keepdims=True), (8, LANES))


def chain_kernel(peers, got, well_sums, order_in, send, step_ref, base_ref, inflow_ref):
    layer = lax.axis_index("layer")
    is_left = iota((peers, LANES), 1) < HALF

    def rows(m, count=4):
        return [got[pl.ds(4 * m + j, peers, PACK), :] for j in range(count)]

    def turn(x):
        return pltpu.roll(x, HALF, 1)

    def chain(base, order):
        for c in range(3):
            base_ref[c] = base[c]
        x = [jnp.zeros((1, LANES), jnp.float32)] * 3
        for d in order:
            at = slice(d, d + 1)
            for c in range(3):
                inflow_ref[c, at, :] = x[c]
            step = [step_ref[e, at, :] for e in range(9)]
            x = [
                (base_ref[i, at, :] + step[3 * i] * x[0]) + (step[3 * i + 1] * x[1] + step[3 * i + 2] * x[2])
                for i in range(3)
            ]
        return [inflow_ref[c] for c in range(3)]

    sets = [swapped(rows(m), (1, 2)) for m in range(4)]
    for e in range(9):
        step_ref[e] = sets[e // 4][e % 4]
    source = sets[TRIAL][:3]
    last = rows(WELLS, 3)
    fourth = pltpu.roll(last[2], LANES - 5 * BLOCK, 1)
    mixed = []
    for pair in sets[2][1:] + [sets[TRIAL][3], swapped(last + [fourth], (1, 2))[0]]:
        mixed += [turn(pair), pair]
    down = chain(source, range(peers))
    up_base = add(source, vec(mixed[:9], [turn(x) for x in down]))
    up = chain(up_base, reversed(range(peers)))
    both = [jnp.where(is_left, a, b) for a, b in zip(down, up)]
    block = iota((peers, LANES), 1) // BLOCK
    parts = []
    for j in range(3):
        factor = jnp.zeros((peers, LANES), jnp.float32)
        for b in range(7):
            w = 7 * j + b
            if w < 18:
                shift = BLOCK * (b + 1 - (0 if w < 9 else 4)) % LANES
                value = both[w % 3]
                factor = jnp.where(block == b + 1, pltpu.roll(value, shift, 1) if shift else value, factor)
        parts.append(jnp.sum(last[j] * factor, axis=0, keepdims=True))
    mine = well_sums[0:1, :]
    one = iota((1, LANES), 1)
    leader = order_in[pl.ds(4 * (layer // ACROSS), 1), :]
    for c in range(3):
        total = jnp.zeros((1, LANES), jnp.float32)
        for j in range(3):
            for b in range(7):
                w = 7 * j + b
                if w < 18 and (w % 9) // 3 == c:
                    total = total + jnp.where(one // BLOCK == b + 1, parts[j], 0.0)
        mine = mine + jnp.where(one == c * ROWS + leader, lane_sum(total), 0.0)
        send[pl.ds(c, peers, BACK), :] = both[c]
    send[pl.ds(3, peers, BACK), :] = jnp.broadcast_to(mine, (peers, LANES))


def sums_kernel(peers, got, sums):
    total = jnp.sum(got[pl.ds(3, peers, BACK), :], axis=0, keepdims=True)
    sums[...] = jnp.broadcast_to(total, (8, LANES))


def solved_kernel(
    areas, nperf, nwell, tiles, counts, inverse, got, cross, state, trial, place_in,
    solved, same_out, block_out, inflow,
):
    well_masks(areas, nperf, nwell, tiles, counts, inverse, same_out, block_out)
    for c in range(3):
        parts = [got[pl.ds(e * BACK + c, GROUPS, ACROSS * BACK), :] for e in range(ACROSS)]
        for i, part in enumerate(swapped(parts, (1, 2, 4))):
            inflow[3 * (i // 4) + c, pl.ds(i % 4, GROUPS, 4), :] = part

    def rows_of(c):
        low, high = inflow[c, 0:8, :], inflow[c, 8:16, :]
        return jnp.concatenate(
            [placed(low, high, place_in[0:8, :]), placed(low, high, place_in[8:16, :])], axis=0
        )

    u = [rows_of(c) for c in range(3)]
    w = [rows_of(3 + c) for c in range(3)]
    for k in range(DEPTH):
        part = add(vec([cross[e, k] for e in range(9)], u), vec([state[e, k] for e in range(9)], w))
        for c in range(3):
            solved[c, k] = trial[c, k] + part[c]


def pair_kernel(mine, other, out):
    region = lax.axis_index("region")
    out[0:1, :] = jnp.where(region == 0, mine[0:1, :], other[0:1, :])
    out[1:8, :] = jnp.where(region == 0, other[1:8, :], mine[1:8, :])


def wells_kernel(near, after, before, across, same, block, solved, well, out, held, sems):
    gathered = jnp.zeros((ROWS, LANES), jnp.float32)
    column = lax.axis_index("column")
    n_column = lax.axis_size("column")
    for by, sums in enumerate((near, after, across, before)):
        at = lax.rem(column + by, n_column)
        for r in range(2):
            gathered = gathered + jnp.where(same[r * n_column + at] > 0.0, sums[r : r + 1, :], 0.0)
    wide = iota((ROWS, LANES), 1)
    totals = [
        jnp.sum(
            jnp.where((wide >= c * ROWS) & (wide < (c + 1) * ROWS), gathered, 0.0),
            axis=1,
            keepdims=True,
        )
        for c in range(3)
    ]
    rate = vec([block[e] for e in range(9)], totals)
    copies = [pltpu.make_async_copy(held.at[c], out.at[c], sems.at[c]) for c in range(3)]
    for c in range(3):
        for k in range(DEPTH):
            held[c, k] = solved[c, k] - (
                well[c, k] * rate[0] + well[3 + c, k] * rate[1] + well[6 + c, k] * rate[2]
            )
        copies[c].start()
    for copy in copies:
        copy.wait()


def f32(*shape):
    return jax.ShapeDtypeStruct(shape, jnp.float32)


VMEM = pl.BlockSpec(memory_space=pltpu.VMEM)
SMEM = pl.BlockSpec(memory_space=pltpu.SMEM)
LONG = pl.CostEstimate(flops=20_000_000, bytes_accessed=8_000_000, transcendentals=0)
FIRST = pl.CostEstimate(flops=20_000_000_000, bytes_accessed=80_000_000, transcendentals=0)


def call(kernel, out_shape, in_specs, scratch=(), cost=None, aliases=None, out_space=None):
    return pl.pallas_call(
        kernel,
        out_shape=out_shape,
        in_specs=in_specs,
        out_specs=jax.tree.map(lambda _: out_space or VMEM, out_shape),
        scratch_shapes=scratch,
        cost_estimate=cost,
        input_output_aliases=aliases or {},
        compiler_params=pltpu.CompilerParams(vmem_limit_bytes=32 * 1024 * 1024),
    )


def moved(value, axis, by):
    count = lax.axis_size(axis)
    return lax.ppermute(value, axis, [(i, (i + by) % count) for i in range(count)])


def exchanged(value, axes):
    return lax.all_to_all(value, axes, split_axis=0, concat_axis=0, tiled=True)


def local(rhs, guess, diag, couple, pivot, lower, upper, well, inverse, tiles, counts):
    peers = lax.axis_size("layer")
    areas = lax.axis_size(AREA)
    cells = (DEPTH, ROWS, LANES)
    x_face, right_face, left_face, top_face, bottom_face = call(
        edges_kernel,
        (
            f32(3 * DEPTH, LANES), f32(ROWS, LANES), f32(ROWS, LANES),
            f32(3, ROWS, LANES), f32(3, ROWS, LANES),
        ),
        [VMEM],
        cost=FIRST,
    )(guess)
    below_in = moved(top_face, "layer", 1)
    above_in = moved(bottom_face, "layer", -1)
    right_in = moved(right_face, "column", 1)
    left_in = moved(left_face, "column", -1)
    x_in = moved(x_face, "region", 1)
    nine, three = f32(9, *cells), f32(3, *cells)
    index = jax.ShapeDtypeStruct((ROWS, LANES), jnp.int32)
    send, cross, state, order, place, rest, inner = call(
        lambda *refs: maps_kernel(areas, tiles.shape[0], *refs),
        (
            f32(peers * PACK, LANES), nine, nine, index, index, f32(2, ROWS, LANES),
            three,
        ),
        [SMEM] + [VMEM] * 8,
        [
            pltpu.VMEM((2, 9, DEPTH, 8, LANES), jnp.float32),
            pltpu.VMEM((45, ROWS, LANES), jnp.float32),
            pltpu.VMEM((ROWS, LANES), jnp.int32),
        ],
        cost=LONG,
    )(tiles, pivot, lower, upper, well, rhs, guess, diag, couple)
    send, trial, well_sums = call(
        trial_kernel,
        (f32(peers * PACK, LANES), three, f32(8, LANES)),
        [VMEM] * 14,
        [pltpu.VMEM((2, 3, DEPTH, 8, LANES), jnp.float32), pltpu.VMEM((6, ROWS, LANES), jnp.float32)],
        aliases={13: 0},
    )(x_in, right_in, left_in, below_in, above_in, inner, couple, pivot, lower, upper, well, order, rest, send)
    got = exchanged(send.reshape(peers, PACK, 1, LANES), "layer").reshape(peers * PACK, LANES)
    back = call(
        lambda *refs: chain_kernel(peers, *refs),
        f32(peers * BACK, LANES),
        [VMEM] * 3,
        [
            pltpu.VMEM((9, peers, LANES), jnp.float32),
            pltpu.VMEM((3, peers, LANES), jnp.float32),
            pltpu.VMEM((3, peers, LANES), jnp.float32),
        ],
    )(got, well_sums, order)
    got = exchanged(back.reshape(peers, BACK, 1, LANES), "layer").reshape(peers * BACK, LANES)
    sums = call(lambda *refs: sums_kernel(peers, *refs), f32(8, LANES), [VMEM])(got)
    near = call(pair_kernel, f32(8, LANES), [VMEM] * 2)(sums, moved(sums, "region", 1))
    after, before, across = [moved(near, "column", by) for by in (-1, 1, 2)]
    solved, same, block = call(
        lambda *refs: solved_kernel(areas, tiles.shape[0], counts.shape[0], *refs),
        (three, f32(areas, ROWS, LANES), f32(9, ROWS, LANES)),
        [SMEM] * 3 + [VMEM] * 5,
        [pltpu.VMEM((6, ROWS, LANES), jnp.float32)],
        cost=LONG,
    )(tiles, counts, inverse, got, cross, state, trial, place)
    return call(
        wells_kernel,
        three,
        [VMEM] * 8,
        [pltpu.VMEM((3, *cells), jnp.float32), pltpu.SemaphoreType.DMA((3,))],
        out_space=pl.BlockSpec(memory_space=pl.ANY),
    )(near, after, before, across, same, block, solved, well)


def solution(mesh):
    cells = P(None, "layer", "region", "column")
    return jax.shard_map(
        local,
        mesh=mesh,
        in_specs=(cells,) * 8 + (P(),) * 3,
        out_specs=cells,
        check_vma=False,
    )
```

```python
import jax
import jax.numpy as jnp
from jax import lax
from jax.experimental import pallas as pl
from jax.experimental.pallas import tpu as pltpu
from jax.sharding import PartitionSpec as P

AREA = ("region", "column")
DEPTH, ROWS, LANES = 8, 16, 128
HALF = LANES // 2
BLOCK = 16
GROUPS, ACROSS = 4, 8
PACK = 19
BACK = 4

TRIAL, WELLS = 3, 4


def mat(a, b):
    return [
        a[3 * i] * b[m] + a[3 * i + 1] * b[3 + m] + a[3 * i + 2] * b[6 + m]
        for i in range(3)
        for m in range(3)
    ]


def vec(a, x):
    return [a[3 * i] * x[0] + a[3 * i + 1] * x[1] + a[3 * i + 2] * x[2] for i in range(3)]


def neg(a):
    return [-entry for entry in a]


def add(a, b):
    return [x + y for x, y in zip(a, b)]


def sub(a, b):
    return [x - y for x, y in zip(a, b)]


def iota(shape, axis):
    return lax.broadcasted_iota(jnp.int32, shape, axis)


def edges_kernel(guess, x_out, right_out, left_out, top_out, bottom_out):
    region = lax.axis_index("region")
    lane = iota((ROWS, LANES), 1)
    right = jnp.zeros((ROWS, LANES), jnp.float32)
    left = jnp.zeros((ROWS, LANES), jnp.float32)
    for c in range(3):
        for k in range(DEPTH):
            place = c * DEPTH + k
            block = guess[c, k]
            right = jnp.where(lane == place, pltpu.roll(block, (place + 1) % LANES, 1), right)
            left = jnp.where(lane == place, pltpu.roll(block, place, 1) if place else block, left)
            x_out[place : place + 1, :] = jnp.where(
                region == 0, guess[c, k, ROWS - 1 :, :], guess[c, k, :1, :]
            )
        top_out[c] = guess[c, DEPTH - 1]
        bottom_out[c] = guess[c, 0]
    right_out[...] = right
    left_out[...] = left


def swapped(parts, steps):
    parts = list(parts)
    for step in steps:
        block = iota(parts[0].shape, 1) // BLOCK
        low = (block & step) == 0
        for i in range(len(parts)):
            if i & step == 0:
                a, b = parts[i], parts[i + step]
                parts[i] = jnp.where(low, a, pltpu.roll(b, BLOCK * step, 1))
                parts[i + step] = jnp.where(low, pltpu.roll(a, LANES - BLOCK * step, 1), b)
    return parts


def placed(low, high, index):
    inner = index & 7
    return jnp.where(
        index < 8,
        jnp.take_along_axis(low, inner, axis=0, mode="promise_in_bounds"),
        jnp.take_along_axis(high, inner, axis=0, mode="promise_in_bounds"),
    )


def put(send, h, m, parts, count=4):
    for e, part in enumerate(swapped(parts, (1, 2, 4))):
        for half in range(2):
            at = (ACROSS * (2 * h + half) + e) * PACK + 4 * m
            send[at : at + count, :] = part[4 * half : 4 * half + count, :]


def lane_sum(x):
    return jnp.sum(x, axis=1, keepdims=True)


def row_order(flag_lane, flag_row, order_out, place_out, group_out):
    row = iota((ROWS, LANES), 0)
    lane = iota((ROWS, LANES), 1)
    inner = lane % ROWS

    def place_of(flag, rank, number):
        free = number - rank
        return jnp.where(flag > 0.0, 4 * rank, free + 1 + ((free * 11) >> 5))

    rank_row = lane_sum(jnp.where((lane < ROWS) & (lane < row), flag_lane, 0.0))
    rank_lane = jnp.sum(jnp.where(row < inner, flag_row, 0.0), axis=0, keepdims=True)
    rank_row = jnp.broadcast_to(rank_row, (ROWS, LANES)).astype(jnp.int32)
    rank_lane = jnp.broadcast_to(rank_lane, (ROWS, LANES)).astype(jnp.int32)
    place_out[...] = place_of(flag_row, rank_row, row)
    at_lane = place_of(flag_lane, rank_lane, inner)
    number = jnp.where(lane < ROWS, lane, 0).astype(jnp.float32)
    for out, wanted in ((order_out, row), (group_out, row & 12)):
        found = lane_sum(jnp.where(at_lane == wanted, number, 0.0))
        out[...] = jnp.broadcast_to(found, (ROWS, LANES)).astype(jnp.int32)


def own_area():
    return lax.axis_index("region") * lax.axis_size("column") + lax.axis_index("column")


def tile_places(areas, nperf, tiles):
    tile_all = iota((areas, LANES), 0) * ROWS + iota((areas, LANES), 1) % ROWS
    tile_own = own_area() * ROWS + iota((ROWS, LANES), 0)
    place_all = jnp.full((areas, LANES), -1, jnp.int32)
    place_own = jnp.full((ROWS, LANES), -1, jnp.int32)
    for p in range(nperf):
        place_all = jnp.where(tile_all == tiles[p], p, place_all)
        place_own = jnp.where(tile_own == tiles[p], p, place_own)
    return place_all, place_own


def well_masks(areas, nperf, nwell, tiles, counts, inverse, same_out, block_out):
    place_all, place_own = tile_places(areas, nperf, tiles)
    well_all = jnp.where(place_all < 0, -1, 0)
    well_own = jnp.where(place_own < 0, -2, 0)
    end = 0
    for w in range(nwell):
        end = end + counts[w]
        well_all = well_all + (place_all >= end).astype(jnp.int32)
        well_own = well_own + (place_own >= end).astype(jnp.int32)
    for a in range(areas):
        same_out[a] = (well_own == well_all[a : a + 1, :]).astype(jnp.float32)
    for e in range(9):
        entry = jnp.zeros((ROWS, LANES), jnp.float32)
        for w in range(nwell):
            entry = jnp.where(well_own == w, inverse[e, w], entry)
        block_out[e] = entry


def maps_kernel(
    areas, nperf, tiles, pivot, lower, upper, well, rhs, guess, diag, couple,
    send, cross_out, state_out, order, place_out, rest, inner, states, maps, group,
):
    place_all, place_own = tile_places(areas, nperf, tiles)
    mine = (iota((areas, LANES), 0) == own_area()) & (place_all >= 0)
    flag_lane = jnp.sum(jnp.where(mine, 1.0, 0.0), axis=0, keepdims=True)
    flag_lane = jnp.broadcast_to(flag_lane, (ROWS, LANES))
    row_order(flag_lane, jnp.where(place_own >= 0, 1.0, 0.0), order, place_out, group)
    top = DEPTH - 1
    halves = [slice(0, 8), slice(8, 16)]

    def load(ref, k, h):
        return [ref[c, k, halves[h], :] for c in range(9)]

    row = iota((8, LANES), 0)
    lane = iota((8, LANES), 1)
    for k in range(DEPTH):
        for h in range(2):
            at = halves[h]
            mid = [guess[c, k, at, :] for c in range(3)]
            out = vec(load(diag, k, h), mid)
            for c in range(3):
                g = mid[c]
                if h == 0:
                    below = jnp.where(row == 0, 0.0, pltpu.roll(g, 1, 0))
                    above = guess[c, k, 1:9, :]
                else:
                    below = guess[c, k, 7:15, :]
                    above = jnp.where(row == 7, 0.0, pltpu.roll(g, 7, 0))
                before = jnp.where(lane == 0, 0.0, pltpu.roll(g, 1, 1))
                after = jnp.where(lane == LANES - 1, 0.0, pltpu.roll(g, LANES - 1, 1))
                beside = below + above + before + after
                if k > 0:
                    beside = beside + guess[c, k - 1, at, :]
                if k < top:
                    beside = beside + guess[c, k + 1, at, :]
                inner[c, k, at, :] = rhs[c, k, at, :] - (out[c] - couple[c, k, at, :] * beside)

    state = [None, None]
    for k in range(DEPTH):
        for h in range(2):
            low = load(lower, k, h)
            state[h] = neg(mat(load(pivot, k, h), low if k == 0 else mat(low, state[h])))
            for c in range(9):
                states[h, c, k] = state[h][c]
    down, cross = list(state), list(state)
    well_state, well_cross = [None, None], [None, None]
    for k in reversed(range(DEPTH)):
        for h in range(2):
            both = mat(load(pivot, k, h), load(upper, k, h))
            if k == top:
                state[h] = neg(both)
            else:
                cross[h] = sub([states[h, c, k] for c in range(9)], mat(both, cross[h]))
                state[h] = neg(mat(both, state[h]))
            coef = load(well, k, h)
            more_state, more_cross = mat(coef, state[h]), mat(coef, cross[h])
            well_state[h] = more_state if k == top else add(well_state[h], more_state)
            well_cross[h] = more_cross if k == top else add(well_cross[h], more_cross)
            for c in range(9):
                cross_out[c, k, halves[h], :] = cross[h][c]
                state_out[c, k, halves[h], :] = state[h][c]
    for h in range(2):
        for e in range(9):
            maps[e, halves[h], :] = down[h][e]
            maps[9 + e, halves[h], :] = state[h][e]
            maps[18 + e, halves[h], :] = cross[h][e]
            maps[27 + e, halves[h], :] = well_cross[h][e]
            maps[36 + e, halves[h], :] = well_state[h][e]
    for h in range(2):
        at = slice(8 * h, 8 * h + 8)

        def take(e, index):
            return placed(maps[e, 0:8, :], maps[e, 8:16, :], index[at, :])

        down = [take(e, order) for e in range(9)]
        state = [take(9 + e, order) for e in range(9)]
        cross = [take(18 + e, order) for e in range(9)]
        wells = [take(27 + e, group) for e in range(18)]
        put(send, h, 0, down[:4] + state[:4])
        put(send, h, 1, down[4:8] + state[4:8])
        put(send, h, 2, [down[8], cross[0], cross[2], cross[4], state[8], cross[1], cross[3], cross[5]])
        rest[0, at, :] = cross[6]
        rest[1, at, :] = cross[7]
        j = iota((8, LANES), 0) & 3
        behind = []
        for b in range(7):
            value = jnp.where(j == 0, wells[b], wells[7 + b])
            third = wells[14 + b] if b < 4 else pltpu.roll(cross[8], 7, 0)
            behind.append(jnp.where(j == 2, third, value) if b < 5 else value)
        put(send, h, WELLS, [cross[8]] + behind, 3)


def trial_kernel(
    x_in, right_in, left_in, below_in, above_in, inner, couple, pivot, lower, upper, well, order, rest, sent,
    send, trial_out, well_out, forward, ends,
):
    region = lax.axis_index("region")
    column = lax.axis_index("column")
    layer = lax.axis_index("layer")
    n_column = lax.axis_size("column")
    n_layer = lax.axis_size("layer")
    lane = iota((8, LANES), 1)
    row = iota((8, LANES), 0)
    top = DEPTH - 1
    well_sums = jnp.zeros((8, LANES), jnp.float32)
    halves = [slice(0, 8), slice(8, 16)]
    edges_right = [jnp.where(column > 0, right_in[at, :], 0.0) for at in halves]
    edges_left = [jnp.where(column < n_column - 1, left_in[at, :], 0.0) for at in halves]

    def load(ref, k, h, count=9):
        return [ref[c, k, halves[h], :] for c in range(count)]

    def residual(k, h):
        at, edge_right, edge_left = halves[h], edges_right[h], edges_left[h]
        out = []
        for c in range(3):
            place = c * DEPTH + k
            x_row = x_in[place : place + 1, :]
            outer = jnp.where(region > 0 if h == 0 else region == 0, x_row, 0.0)
            beside = jnp.where(row == (0 if h == 0 else 7), outer, 0.0)
            first = pltpu.roll(edge_right, LANES - place, 1) if place else edge_right
            last = pltpu.roll(edge_left, LANES - 1 - place, 1)
            ends_y = jnp.where(lane == 0, first, jnp.where(lane == LANES - 1, last, 0.0))
            beside = beside + ends_y
            if k == 0:
                beside = beside + jnp.where(layer > 0, below_in[c, at, :], 0.0)
            if k == top:
                beside = beside + jnp.where(layer < n_layer - 1, above_in[c, at, :], 0.0)
            out.append(inner[c, k, at, :] + couple[c, k, at, :] * beside)
        return out

    f = [None, None]
    for k in range(DEPTH):
        for h in range(2):
            res = residual(k, h)
            if k > 0:
                res = sub(res, vec(load(lower, k, h), f[h]))
            f[h] = vec(load(pivot, k, h), res)
            for c in range(3):
                forward[h, c, k] = f[h][c]
    s, well_const = list(f), [None, None]
    for k in reversed(range(DEPTH)):
        for h in range(2):
            if k < top:
                more = vec(load(pivot, k, h), vec(load(upper, k, h), s[h]))
                s[h] = sub([forward[h, c, k] for c in range(3)], more)
            more = vec(load(well, k, h), s[h])
            well_const[h] = more if k == top else add(well_const[h], more)
            for c in range(3):
                trial_out[c, k, halves[h], :] = s[h][c]
    for h in range(2):
        for c in range(3):
            ends[c, halves[h], :] = f[h][c]
            ends[3 + c, halves[h], :] = s[h][c]
            total = lane_sum(well_const[h][c])
            well_sums = well_sums + jnp.where(lane == c * ROWS + 8 * h + row, total, 0.0)
    for h in range(2):
        at = slice(8 * h, 8 * h + 8)
        source = [placed(ends[c, 0:8, :], ends[c, 8:16, :], order[at, :]) for c in range(6)]
        put(send, h, TRIAL, source[:3] + [rest[0, at, :]] + source[3:] + [rest[1, at, :]])
    well_out[...] = jnp.broadcast_to(jnp.sum(well_sums, axis=0, keepdims=True), (8, LANES))


def chain_kernel(peers, got, well_sums, order_in, send, step_ref, base_ref, inflow_ref):
    layer = lax.axis_index("layer")
    is_left = iota((peers, LANES), 1) < HALF

    def rows(m, count=4):
        return [got[pl.ds(4 * m + j, peers, PACK), :] for j in range(count)]

    def turn(x):
        return pltpu.roll(x, HALF, 1)

    def chain(base, order):
        for c in range(3):
            base_ref[c] = base[c]
        x = [jnp.zeros((1, LANES), jnp.float32)] * 3
        for d in order:
            at = slice(d, d + 1)
            for c in range(3):
                inflow_ref[c, at, :] = x[c]
            step = [step_ref[e, at, :] for e in range(9)]
            x = [
                (base_ref[i, at, :] + step[3 * i] * x[0]) + (step[3 * i + 1] * x[1] + step[3 * i + 2] * x[2])
                for i in range(3)
            ]
        return [inflow_ref[c] for c in range(3)]

    sets = [swapped(rows(m), (1, 2)) for m in range(4)]
    for e in range(9):
        step_ref[e] = sets[e // 4][e % 4]
    source = sets[TRIAL][:3]
    last = rows(WELLS, 3)
    fourth = pltpu.roll(last[2], LANES - 5 * BLOCK, 1)
    mixed = []
    for pair in sets[2][1:] + [sets[TRIAL][3], swapped(last + [fourth], (1, 2))[0]]:
        mixed += [turn(pair), pair]
    down = chain(source, range(peers))
    up_base = add(source, vec(mixed[:9], [turn(x) for x in down]))
    up = chain(up_base, reversed(range(peers)))
    both = [jnp.where(is_left, a, b) for a, b in zip(down, up)]
    block = iota((peers, LANES), 1) // BLOCK
    parts = []
    for j in range(3):
        factor = jnp.zeros((peers, LANES), jnp.float32)
        for b in range(7):
            w = 7 * j + b
            if w < 18:
                shift = BLOCK * (b + 1 - (0 if w < 9 else 4)) % LANES
                value = both[w % 3]
                factor = jnp.where(block == b + 1, pltpu.roll(value, shift, 1) if shift else value, factor)
        parts.append(jnp.sum(last[j] * factor, axis=0, keepdims=True))
    mine = well_sums[0:1, :]
    one = iota((1, LANES), 1)
    leader = order_in[pl.ds(4 * (layer // ACROSS), 1), :]
    for c in range(3):
        total = jnp.zeros((1, LANES), jnp.float32)
        for j in range(3):
            for b in range(7):
                w = 7 * j + b
                if w < 18 and (w % 9) // 3 == c:
                    total = total + jnp.where(one // BLOCK == b + 1, parts[j], 0.0)
        mine = mine + jnp.where(one == c * ROWS + leader, lane_sum(total), 0.0)
        send[pl.ds(c, peers, BACK), :] = both[c]
    send[pl.ds(3, peers, BACK), :] = jnp.broadcast_to(mine, (peers, LANES))


def sums_kernel(peers, got, sums):
    total = jnp.sum(got[pl.ds(3, peers, BACK), :], axis=0, keepdims=True)
    sums[...] = total


def solved_kernel(
    areas, nperf, nwell, tiles, counts, inverse, got, cross, state, trial, place_in,
    solved, same_out, block_out, inflow,
):
    well_masks(areas, nperf, nwell, tiles, counts, inverse, same_out, block_out)
    for c in range(3):
        parts = [got[pl.ds(e * BACK + c, GROUPS, ACROSS * BACK), :] for e in range(ACROSS)]
        for i, part in enumerate(swapped(parts, (1, 2, 4))):
            inflow[3 * (i // 4) + c, pl.ds(i % 4, GROUPS, 4), :] = part

    def rows_of(c):
        low, high = inflow[c, 0:8, :], inflow[c, 8:16, :]
        return jnp.concatenate(
            [placed(low, high, place_in[0:8, :]), placed(low, high, place_in[8:16, :])], axis=0
        )

    u = [rows_of(c) for c in range(3)]
    w = [rows_of(3 + c) for c in range(3)]
    for k in range(DEPTH):
        part = add(vec([cross[e, k] for e in range(9)], u), vec([state[e, k] for e in range(9)], w))
        for c in range(3):
            solved[c, k] = trial[c, k] + part[c]


def pair_kernel(mine, other, out):
    region = lax.axis_index("region")
    out[0:1, :] = jnp.where(region == 0, mine[...], other[...])
    out[1:2, :] = jnp.where(region == 0, other[...], mine[...])


def wells_kernel(near, after, before, across, same, block, solved, well, out, held, sems):
    gathered = jnp.zeros((ROWS, LANES), jnp.float32)
    column = lax.axis_index("column")
    n_column = lax.axis_size("column")
    for by, sums in enumerate((near, after, across, before)):
        at = lax.rem(column + by, n_column)
        for r in range(2):
            gathered = gathered + jnp.where(same[r * n_column + at] > 0.0, sums[r : r + 1, :], 0.0)
    wide = iota((ROWS, LANES), 1)
    totals = [
        jnp.sum(
            jnp.where((wide >= c * ROWS) & (wide < (c + 1) * ROWS), gathered, 0.0),
            axis=1,
            keepdims=True,
        )
        for c in range(3)
    ]
    rate = vec([block[e] for e in range(9)], totals)
    copies = [pltpu.make_async_copy(held.at[c], out.at[c], sems.at[c]) for c in range(3)]
    for c in range(3):
        for k in range(DEPTH):
            held[c, k] = solved[c, k] - (
                well[c, k] * rate[0] + well[3 + c, k] * rate[1] + well[6 + c, k] * rate[2]
            )
        copies[c].start()
    for copy in copies:
        copy.wait()


def f32(*shape):
    return jax.ShapeDtypeStruct(shape, jnp.float32)


VMEM = pl.BlockSpec(memory_space=pltpu.VMEM)
SMEM = pl.BlockSpec(memory_space=pltpu.SMEM)
LONG = pl.CostEstimate(flops=20_000_000, bytes_accessed=8_000_000, transcendentals=0)
FIRST = pl.CostEstimate(flops=20_000_000_000, bytes_accessed=80_000_000, transcendentals=0)


def call(kernel, out_shape, in_specs, scratch=(), cost=None, aliases=None, out_space=None):
    return pl.pallas_call(
        kernel,
        out_shape=out_shape,
        in_specs=in_specs,
        out_specs=jax.tree.map(lambda _: out_space or VMEM, out_shape),
        scratch_shapes=scratch,
        cost_estimate=cost,
        input_output_aliases=aliases or {},
        compiler_params=pltpu.CompilerParams(vmem_limit_bytes=32 * 1024 * 1024),
    )


def moved(value, axis, by):
    count = lax.axis_size(axis)
    return lax.ppermute(value, axis, [(i, (i + by) % count) for i in range(count)])


def exchanged(value, axes):
    return lax.all_to_all(value, axes, split_axis=0, concat_axis=0, tiled=True)


def local(rhs, guess, diag, couple, pivot, lower, upper, well, inverse, tiles, counts):
    peers = lax.axis_size("layer")
    areas = lax.axis_size(AREA)
    cells = (DEPTH, ROWS, LANES)
    x_face, right_face, left_face, top_face, bottom_face = call(
        edges_kernel,
        (
            f32(3 * DEPTH, LANES), f32(ROWS, LANES), f32(ROWS, LANES),
            f32(3, ROWS, LANES), f32(3, ROWS, LANES),
        ),
        [VMEM],
        cost=FIRST,
    )(guess)
    below_in = moved(top_face, "layer", 1)
    above_in = moved(bottom_face, "layer", -1)
    right_in = moved(right_face, "column", 1)
    left_in = moved(left_face, "column", -1)
    x_in = moved(x_face, "region", 1)
    nine, three = f32(9, *cells), f32(3, *cells)
    index = jax.ShapeDtypeStruct((ROWS, LANES), jnp.int32)
    send, cross, state, order, place, rest, inner = call(
        lambda *refs: maps_kernel(areas, tiles.shape[0], *refs),
        (
            f32(peers * PACK, LANES), nine, nine, index, index, f32(2, ROWS, LANES),
            three,
        ),
        [SMEM] + [VMEM] * 8,
        [
            pltpu.VMEM((2, 9, DEPTH, 8, LANES), jnp.float32),
            pltpu.VMEM((45, ROWS, LANES), jnp.float32),
            pltpu.VMEM((ROWS, LANES), jnp.int32),
        ],
        cost=LONG,
    )(tiles, pivot, lower, upper, well, rhs, guess, diag, couple)
    send, trial, well_sums = call(
        trial_kernel,
        (f32(peers * PACK, LANES), three, f32(8, LANES)),
        [VMEM] * 14,
        [pltpu.VMEM((2, 3, DEPTH, 8, LANES), jnp.float32), pltpu.VMEM((6, ROWS, LANES), jnp.float32)],
        aliases={13: 0},
    )(x_in, right_in, left_in, below_in, above_in, inner, couple, pivot, lower, upper, well, order, rest, send)
    got = exchanged(send.reshape(peers, PACK, 1, LANES), "layer").reshape(peers * PACK, LANES)
    back = call(
        lambda *refs: chain_kernel(peers, *refs),
        f32(peers * BACK, LANES),
        [VMEM] * 3,
        [
            pltpu.VMEM((9, peers, LANES), jnp.float32),
            pltpu.VMEM((3, peers, LANES), jnp.float32),
            pltpu.VMEM((3, peers, LANES), jnp.float32),
        ],
    )(got, well_sums, order)
    got = exchanged(back.reshape(peers, BACK, 1, LANES), "layer").reshape(peers * BACK, LANES)
    sums = call(lambda *refs: sums_kernel(peers, *refs), f32(1, LANES), [VMEM])(got)
    near = call(pair_kernel, f32(2, LANES), [VMEM] * 2)(sums, moved(sums, "region", 1))
    after, before, across = [moved(near, "column", by) for by in (-1, 1, 2)]
    solved, same, block = call(
        lambda *refs: solved_kernel(areas, tiles.shape[0], counts.shape[0], *refs),
        (three, f32(areas, ROWS, LANES), f32(9, ROWS, LANES)),
        [SMEM] * 3 + [VMEM] * 5,
        [pltpu.VMEM((6, ROWS, LANES), jnp.float32)],
        cost=LONG,
    )(tiles, counts, inverse, got, cross, state, trial, place)
    return call(
        wells_kernel,
        three,
        [VMEM] * 8,
        [pltpu.VMEM((3, *cells), jnp.float32), pltpu.SemaphoreType.DMA((3,))],
        out_space=pl.BlockSpec(memory_space=pl.ANY),
    )(near, after, before, across, same, block, solved, well)


def solution(mesh):
    cells = P(None, "layer", "region", "column")
    return jax.shard_map(
        local,
        mesh=mesh,
        in_specs=(cells,) * 8 + (P(),) * 3,
        out_specs=cells,
        check_vma=False,
    )
```
